256 devices in a mesh: wide: 32 (over z_lo, x, core), depth: 8 (over z_hi, y).
Axes of the slice: x: 4, y: 4, z: 8 (z_hi: 2, z_lo: 4; z = z_hi * 4 + z_lo), core: 2. Of those that a mesh axis runs over, the one named last changes fastest.
Arguments:
- attn_out: bfloat16 [8192, 4096], P('wide', 'depth'), may hold values from -6 to 6
- resid: bfloat16 [8192, 4096], P('wide'), may hold values from -6 to 6
- out_proj: bfloat16 [4096, 4096], P('wide', 'depth'), may hold values from -0.09375 to 0.09375
- section_in: bfloat16 [8, 4096, 1024], P('depth', 'wide'), may hold values from -0.09375 to 0.09375
- codebook: bfloat16 [8, 2048, 1024], P('depth'), may hold values from -6 to 6
- decays: float32 [8, 1024], P('depth'), may hold values from 0.001 to 1
- section_out: bfloat16 [8, 1024, 2048], P('depth'), may hold values from -16 to 16
- codes: int32 [8, 8192], P(None, 'wide'), may hold values from 0 to 2047
Outputs:
- losses: float32 [8, 8192], P('depth', 'wide')
- grad_out_proj: bfloat16 [4096, 4096], P('wide', 'depth')
The draws below stay inside these ranges and needn't reach their ends.
All inputs are finite; a program needn't handle non-finite values.
Results may differ from the reference program's by a relative error of at most 0.03.
Values may be sent and summed in bfloat16 or wider, within the bound.
A program may use at most 128 MiB of HBM per device.

```python
import math
import jax
import jax.numpy as jnp
from jax import lax

D = 4096
DD = 1024
CODES = 2048
QUANTIZER_TOTAL = 8
LENGTH = 256
FR_DEV = 256
FRAMES = 8192


def draw_decays(key, part):
    key = jax.random.fold_in(key, 11)
    seed_frequency_sample, seed_perturbation, seed_spike_sample, seed_threshold = jax.random.split(key, 4)
    low_rate = 0.02
    high_rate = 3.0
    log_rates = jax.random.uniform(seed_frequency_sample, (1, DD), jnp.float32, math.log(low_rate), math.log(high_rate))
    jitter = jax.random.uniform(seed_perturbation, (QUANTIZER_TOTAL, DD), jnp.float32, -0.7, 0.7)
    rates = jnp.exp(log_rates + jitter)
    spike_occurrences = jax.random.randint(seed_spike_sample, (2,), 0, QUANTIZER_TOTAL)
    quantizer_ordinals = jnp.arange(QUANTIZER_TOTAL, dtype=jnp.int32)[:, None]
    affected_indicator = jnp.logical_or(quantizer_ordinals == spike_occurrences[0], quantizer_ordinals == spike_occurrences[1])
    cut_factor = jax.random.uniform(seed_threshold, (QUANTIZER_TOTAL, DD), jnp.float32, 0.5, 0.8)
    return jnp.exp(-rates) * jnp.where(affected_indicator, cut_factor, 1.0)


def draw_section_out(key, part):
    key = jax.random.fold_in(key, 23)
    key_base = jax.random.fold_in(key, 0)
    values = jnp.clip(0.1 * jax.random.normal(key_base, (QUANTIZER_TOTAL, DD, CODES), jnp.float32), -0.8, 0.8)
    return values.astype(jnp.bfloat16)


def with_ends(drawn, key, least, high):
    longest = drawn.shape.index(max(drawn.shape))
    spots = []
    for shift in (0, 1):
        where = [jax.random.randint(jax.random.fold_in(key, axis), (), 0, length) for axis, length in enumerate(drawn.shape)]
        where[longest] = (where[longest] + shift) % drawn.shape[longest]
        spots.append(tuple(where))
    return drawn.at[spots[0]].set(least).at[spots[1]].set(high)


def block_scale(rng, shape, pieces, smallest, high):
    factor_of = 1.0
    for dim, shards_of in pieces:
        heights = jax.random.uniform(jax.random.fold_in(jax.random.fold_in(rng, 6), dim), (shards_of,), jnp.float32, smallest / len(pieces), high / len(pieces))
        factor_of = factor_of * jnp.repeat(jnp.exp(heights), shape[dim] // shards_of).reshape((-1,) + (1,) * (len(shape) - 1 - dim))
    return factor_of


def noise(rng, shape, width, limit, cuts=(), kind=jnp.bfloat16):
    result = width * jax.random.normal(rng, shape, jnp.float32)
    if cuts:
        result = result * block_scale(rng, shape, cuts, -0.22, 0.18)
    return jnp.clip(result, -limit, limit).astype(kind)


def setup_inputs(seed: int = 0) -> dict:
    seeds = jax.random.split(jax.random.key(seed), 9)
    attn_out = noise(seeds[0], (FRAMES, D), 1.0, 6.0, ((0, 32), (1, 8)))
    resid = noise(seeds[1], (FRAMES, D), 1.0, 6.0, ((0, 32),))
    out_proj = noise(seeds[2], (D, D), D ** -0.5, 0.09375, ((0, 32), (1, 8)))
    section_in = noise(seeds[3], (QUANTIZER_TOTAL, D, DD), D ** -0.5, 0.09375, ((0, 8), (1, 32)))
    codebook = noise(seeds[4], (QUANTIZER_TOTAL, CODES, DD), 1.0, 6.0, ((0, 8),))
    decays = draw_decays(jax.random.fold_in(seeds[8], 71), 0)
    section_out = draw_section_out(jax.random.fold_in(seeds[8], 71), 0)
    codes = with_ends(jax.random.randint(seeds[7], (QUANTIZER_TOTAL, FRAMES), 0, CODES), jax.random.fold_in(seeds[7], 1), 0, CODES - 1).astype(jnp.int32)
    return {"attn_out": attn_out, "resid": resid, "out_proj": out_proj, "section_in": section_in, "codebook": codebook, "decays": decays, "section_out": section_out, "codes": codes}


epsilon = 1e-06

def inverse_rms(values):
    return lax.rsqrt(lax.optimization_barrier(jnp.mean(values * values, axis=-1, keepdims=True)) + epsilon)

def rms_backward(values, upstream):
    factor = inverse_rms(values)
    inner = lax.optimization_barrier(jnp.mean(upstream * values, axis=-1, keepdims=True))
    return factor * upstream - values * (factor * factor * factor) * inner

def previous_codes(codes):
    shifted = jnp.concatenate([jnp.zeros((1,), jnp.int32), codes[-1, :-1].astype(jnp.int32)])
    return jnp.concatenate([shifted[None, :], codes[:-1].astype(jnp.int32)], axis=0)

def reference(attn_out, resid, out_proj, section_in, codebook, decays, section_out, codes):
    mixed = jnp.dot(attn_out, out_proj.T, preferred_element_type=jnp.float32)
    pre = resid.astype(jnp.float32) + mixed
    context = (pre * inverse_rms(pre)).astype(jnp.bfloat16)
    previous = previous_codes(codes)
    positions = jnp.arange(FRAMES, dtype=jnp.int32) % LENGTH
    columns = jnp.arange(CODES, dtype=jnp.int32)
    state = jnp.zeros((FRAMES, DD), jnp.float32)
    loss_rows = []
    local_grads = []
    for section_index in range(QUANTIZER_TOTAL):
        embedded = jnp.take(codebook[section_index], previous[section_index], axis=0).astype(jnp.float32)
        if section_index == 0:
            embedded = embedded * (positions != 0).astype(jnp.float32)[:, None]
        inputs = jnp.dot(context, section_in[section_index], preferred_element_type=jnp.float32) + embedded
        state = decays[section_index] * state + inputs
        normed = (state * inverse_rms(state)).astype(jnp.bfloat16)
        logits = jnp.dot(normed, section_out[section_index], preferred_element_type=jnp.float32)
        total_log = jax.nn.logsumexp(logits, axis=1)
        chosen = columns[None, :] == codes[section_index][:, None]
        picked = lax.optimization_barrier(jnp.sum(jnp.where(chosen, logits, 0.0), axis=1))
        loss_rows.append(total_log - picked)
        probs = jnp.exp(logits - total_log[:, None])
        dlogits = (probs - chosen.astype(jnp.float32)).astype(jnp.bfloat16)
        grad_normed = jnp.dot(dlogits, section_out[section_index].T, preferred_element_type=jnp.float32)
        local_grads.append(rms_backward(state, grad_normed))
    carried = jnp.zeros((FRAMES, DD), jnp.float32)
    grad_context = jnp.zeros((FRAMES, D), jnp.float32)
    for section_index in reversed(range(QUANTIZER_TOTAL)):
        grad_here = local_grads[section_index] + carried
        grad_context = grad_context + jnp.dot(grad_here.astype(jnp.bfloat16), section_in[section_index].T, preferred_element_type=jnp.float32)
        carried = decays[section_index] * grad_here
    grad_pre = rms_backward(pre, grad_context).astype(jnp.bfloat16)

    def add_block(running, block_index):
        block_grad = lax.dynamic_slice_in_dim(grad_pre, block_index * FR_DEV, FR_DEV, 0)
        block_attn = lax.dynamic_slice_in_dim(attn_out, block_index * FR_DEV, FR_DEV, 0)
        term = jnp.dot(block_grad.T, block_attn, preferred_element_type=jnp.float32)
        rounded = lax.optimization_barrier(term.astype(jnp.bfloat16))
        return (running + rounded.astype(jnp.float32), None)
    blocks = jnp.arange(FRAMES // FR_DEV, dtype=jnp.int32)
    summed, _ = lax.scan(add_block, jnp.zeros((D, D), jnp.float32), blocks)
    return (jnp.stack(loss_rows), summed.astype(jnp.bfloat16))
```

```python
import functools

import jax
import jax.numpy as jnp
from jax import lax
from jax.experimental import pallas as pl
from jax.experimental.pallas import tpu as pltpu
from jax.sharding import PartitionSpec as P

MESH = pl.DeviceIdType.MESH
LENGTH = 256
EPSILON = 1e-06
BF = jnp.bfloat16
F32 = jnp.float32
VMEM_LIMIT = 50 << 20
NT = (((1,), (1,)), ((), ()))


class Place:
    def __init__(self):
        w, d = lax.axis_index("wide"), lax.axis_index("depth")
        self.zl, self.x, self.c = w // 8, (w // 2) % 4, w % 2
        self.zh, self.y = d // 4, d % 4
        self.d = d

    def at(self, zl=None, x=None, c=None, zh=None, y=None):
        zl = self.zl if zl is None else zl
        x = self.x if x is None else x
        c = self.c if c is None else c
        zh = self.zh if zh is None else zh
        y = self.y if y is None else y
        return (zl * 8 + x * 2 + c, zh * 4 + y)

    def ys(self):
        return [(self.y + k) % 4 for k in (2, 1, 3)]

    def xs(self):
        return [(self.x + k) % 4 for k in (2, 1, 3)]

    def zls(self):
        return [(self.zl + k) % 4 for k in (2, 1, 3)]

    def to_features(self):
        return self.at(
            zh=self.zl // 2,
            y=(self.zl % 2) * 2 + self.x // 2,
            zl=(self.x % 2) * 2 + self.zh,
            x=self.y,
            c=1 - self.c,
        )

    def to_owner(self):
        return self.at(
            zl=self.zh * 2 + self.y // 2,
            x=(self.y % 2) * 2 + self.zl // 2,
            c=1 - self.c,
            zh=self.zl % 2,
            y=self.x,
        )


class Copies:
    def __init__(self, send_sem, recv_sem):
        self.send_sem, self.recv_sem = send_sem, recv_sem
        self.used = 0
        self.sent = []

    def send(self, source, target, device):
        copy = pltpu.make_async_remote_copy(
            src_ref=source,
            dst_ref=target,
            send_sem=self.send_sem.at[self.used],
            recv_sem=self.recv_sem.at[self.used],
            device_id=device,
            device_id_type=MESH,
        )
        self.used += 1
        copy.start()
        self.sent.append(copy)
        return copy

    def finish(self):
        for copy in self.sent:
            copy.wait_send()


def greet(senders, targets):
    barrier = pltpu.get_barrier_semaphore()
    for device in senders:
        pl.semaphore_signal(barrier, inc=1, device_id=device, device_id_type=MESH)
    pl.semaphore_wait(barrier, len(targets))


def columns(d, width):
    return pl.ds(pl.multiple_of(d * width, width), width)


def front_kernel(
    attn_ref, resid_ref, proj_ref, sec_ref, dec_ref,
    pre_ref, mine_ref, sect_ref, full_ref, decs_ref,
    wd, resid_part, send_sem, recv_sem, local_sem,
):
    me = Place()
    copies = Copies(send_sem, recv_sem)
    width = attn_ref.shape[1]
    own = columns(me.d, width)
    across = columns((1 - me.zh) * 4 + me.y, width)
    resid_copy = pltpu.make_async_copy(resid_ref.at[:, own], resid_part, local_sem.at[0])
    resid_copy.start()
    decs_ref[me.y] = jnp.broadcast_to(dec_ref[...], decs_ref.shape[1:])
    sect_ref[me.zl, me.x, me.c] = sec_ref[...]
    full_ref[:, own] = attn_ref[...]
    y_peers = [me.at(y=y) for y in me.ys()]
    zl_peers = [me.at(zl=zl) for zl in me.zls()]
    right, left = me.at(x=(me.x + 1) % 4), me.at(x=(me.x + 3) % 4)
    far, other = me.at(zh=1 - me.zh), me.at(c=1 - me.c)
    shared = y_peers + zl_peers + [right, left, far, other]
    greet(shared + [me.to_owner()], shared + [me.to_features()])

    dest = me.to_features()
    f_zl, f_x, f_c = dest[0] // 8, (dest[0] // 2) % 4, dest[0] % 2
    moved = copies.send(proj_ref, wd.at[f_zl, f_x, f_c], dest)
    attn_far = copies.send(attn_ref, full_ref.at[:, own], far)
    attn_near = [copies.send(attn_ref, full_ref.at[:, own], peer) for peer in y_peers]
    dec_near = [copies.send(decs_ref.at[me.y], decs_ref.at[me.y], peer) for peer in y_peers]

    moved.wait_recv()
    mine_wd = wd.at[me.zl, me.x, me.c]
    wd_z = [copies.send(mine_wd, mine_wd, peer) for peer in zl_peers]
    sec_slot = sect_ref.at[me.zl, me.x, me.c]
    sec_z = [copies.send(sec_ref, sec_slot, peer) for peer in zl_peers]
    attn_far.wait_recv()
    attn_far_near = [copies.send(full_ref.at[:, across], full_ref.at[:, across], peer) for peer in y_peers]

    def ring_first(buffer):
        group = buffer.at[:, me.x, me.c]
        to_right = copies.send(group, group, right)
        to_left = copies.send(group, group, left)
        to_other = copies.send(group, group, other)
        return to_right, to_left, to_other

    def ring_second(buffer, to_right, to_left):
        to_right.wait_recv()
        from_left = (me.x + 3) % 4
        half = buffer.at[pl.ds(0, 2), from_left, me.c]
        on_right = copies.send(half, half, right)
        group = buffer.at[:, from_left, me.c]
        other_a = copies.send(group, group, other)
        to_left.wait_recv()
        from_right = (me.x + 1) % 4
        half = buffer.at[pl.ds(2, 2), from_right, me.c]
        on_left = copies.send(half, half, left)
        group = buffer.at[:, from_right, me.c]
        other_b = copies.send(group, group, other)
        return on_right, on_left, other_a, other_b

    def ring_third(buffer, on_right, on_left):
        on_right.wait_recv()
        on_left.wait_recv()
        group = buffer.at[:, (me.x + 2) % 4, me.c]
        return copies.send(group, group, other)

    for copy in wd_z:
        copy.wait_recv()
    w1 = ring_first(wd)
    w2 = ring_second(wd, w1[0], w1[1])
    for copy in sec_z:
        copy.wait_recv()
    s1 = ring_first(sect_ref)
    w3 = ring_third(wd, w2[0], w2[1])
    for copy in [w1[2], w2[2], w2[3], w3] + attn_near + attn_far_near:
        copy.wait_recv()
    resid_copy.wait()

    block = proj_ref.shape[0]
    for u in range(2):
        total = jnp.zeros((attn_ref.shape[0], 2 * block), F32)
        for head in range(8):
            weight = wd[u * 2 + head // 4, head % 4].reshape(2 * block, width)
            total += lax.dot_general(
                full_ref[:, head * width : (head + 1) * width], weight, NT, preferred_element_type=F32
            )
        for c in range(2):
            feature = (2 * u + 1 - c) * block
            part = resid_part[:, feature : feature + block].astype(F32) + total[:, c * block : (c + 1) * block]
            mine_ref[:, feature : feature + block] = part.astype(BF)
    pre_ref[:, own] = mine_ref[...]

    pre_far = copies.send(mine_ref, pre_ref.at[:, own], far)
    pre_near = [copies.send(mine_ref, pre_ref.at[:, own], peer) for peer in y_peers]
    s2 = ring_second(sect_ref, s1[0], s1[1])
    pre_far.wait_recv()
    pre_far_near = [copies.send(pre_ref.at[:, across], pre_ref.at[:, across], peer) for peer in y_peers]
    s3 = ring_third(sect_ref, s2[0], s2[1])
    for copy in pre_near + pre_far_near + dec_near + [s1[2], s2[2], s2[3], s3]:
        copy.wait_recv()
    copies.finish()


def front(attn_out, resid, out_proj, section_in, decays):
    frames, width = attn_out.shape
    block, inner = section_in.shape
    vmem = pl.BlockSpec(memory_space=pltpu.VMEM)
    return pl.pallas_call(
        front_kernel,
        out_shape=(
            jax.ShapeDtypeStruct((frames, 8 * width), BF),
            jax.ShapeDtypeStruct((frames, width), BF),
            jax.ShapeDtypeStruct((4, 4, 2, block, inner), BF),
            jax.ShapeDtypeStruct((frames, 8 * width), BF),
            jax.ShapeDtypeStruct((4, 8, inner), F32),
        ),
        in_specs=[vmem, pl.BlockSpec(memory_space=pl.ANY), vmem, vmem, vmem],
        out_specs=[vmem] * 5,
        scratch_shapes=[
            pltpu.VMEM((4, 4, 2) + out_proj.shape, BF),
            pltpu.VMEM((frames, width), BF),
            pltpu.SemaphoreType.DMA((48,)),
            pltpu.SemaphoreType.DMA((48,)),
            pltpu.SemaphoreType.DMA((1,)),
        ],
        compiler_params=pltpu.CompilerParams(
            collective_id=0, has_side_effects=True, vmem_limit_bytes=VMEM_LIMIT
        ),
        name="front",
    )(attn_out, resid, out_proj, section_in, decays)


def scan_kernel(
    backward, in_ref, dec_ref, out_ref, got, done, carry_in, carry_out, send_sem, recv_sem, carry_send, carry_recv
):
    me = Place()
    copies = Copies(send_sem, recv_sem)
    rows = got.shape[1]
    carry_in[...] = jnp.zeros_like(carry_in)
    y_peers = [me.at(y=y) for y in me.ys()]
    far = me.at(zh=1 - me.zh)
    greet(y_peers + [far], y_peers + [far])
    first = 1 if backward else 0

    def part(y):
        return pl.ds(pl.multiple_of(y * rows, rows), rows)

    there = [copies.send(in_ref.at[part(y)], got.at[me.y], me.at(y=y)) for y in me.ys()]
    got[me.y] = in_ref[part(me.y)]
    for copy in there:
        copy.wait_recv()
    carry = pltpu.make_async_remote_copy(
        src_ref=carry_out,
        dst_ref=carry_in,
        send_sem=carry_send.at[0],
        recv_sem=carry_recv.at[0],
        device_id=far,
        device_id_type=MESH,
    )

    @pl.when(me.zh != first)
    def _():
        carry.wait_recv()

    state = carry_in[...].astype(F32)
    for section in reversed(range(4)) if backward else range(4):
        decay = dec_ref[section, 0:1]
        if backward:
            here = got[section].astype(F32) + state
            done[section] = here.astype(BF)
            state = decay * here
        else:
            state = decay * state + got[section].astype(F32)
            done[section] = state.astype(BF)
    carry_out[...] = state.astype(BF)

    @pl.when(me.zh == first)
    def _():
        carry.start()

    back = [copies.send(done.at[y], out_ref.at[part(me.y)], me.at(y=y)) for y in me.ys()]
    out_ref[part(me.y)] = done[me.y]
    for copy in back:
        copy.wait_recv()
    copies.finish()

    @pl.when(me.zh == first)
    def _():
        carry.wait_send()


def scan(backward, values, decays):
    frames, inner = values.shape
    vmem = pl.BlockSpec(memory_space=pltpu.VMEM)
    rows = frames // 4
    return pl.pallas_call(
        functools.partial(scan_kernel, backward),
        out_shape=jax.ShapeDtypeStruct((frames, inner), BF),
        in_specs=[vmem] * 2,
        out_specs=vmem,
        scratch_shapes=[
            pltpu.VMEM((4, rows, inner), BF),
            pltpu.VMEM((4, rows, inner), BF),
            pltpu.VMEM((rows, inner), BF),
            pltpu.VMEM((rows, inner), BF),
            pltpu.SemaphoreType.DMA((6,)),
            pltpu.SemaphoreType.DMA((6,)),
            pltpu.SemaphoreType.DMA((1,)),
            pltpu.SemaphoreType.DMA((1,)),
        ],
        compiler_params=pltpu.CompilerParams(
            collective_id=2 if backward else 1, has_side_effects=True, vmem_limit_bytes=VMEM_LIMIT
        ),
        name="scan_back" if backward else "scan",
    )(values, decays)


def back_kernel(
    grad_ref, inner_ref, mine_ref, factor_ref, full_ref, out_ref,
    got, far_out, far_in, inners, gp, core_got, group, group_got, line, line_got, last,
    send_sem, recv_sem,
):
    me = Place()
    copies = Copies(send_sem, recv_sem)
    frames, width = mine_ref.shape
    block = out_ref.shape[0]
    y_peers = [me.at(y=y) for y in me.ys()]
    x_peers = [me.at(x=x) for x in me.xs()]
    zl_peers = [me.at(zl=zl) for zl in me.zls()]
    far, other = me.at(zh=1 - me.zh), me.at(c=1 - me.c)
    cross = [me.at(zh=1 - me.zh, y=y) for y in me.ys()]
    shared = y_peers + x_peers + zl_peers + cross + [far, other]
    greet(shared + [me.to_features()], shared + [me.to_owner()])

    inner_sent = [copies.send(inner_ref, inners.at[me.d], peer) for peer in y_peers + [far] + cross]
    inners[me.d] = inner_ref[...]

    def cols(zh, y):
        return columns(zh * 4 + y, width)

    first = [
        copies.send(grad_ref.at[:, cols(1 - me.zh, y)], got.at[0, slot], me.at(y=y))
        for slot, y in enumerate(me.ys())
    ]
    second = [
        copies.send(grad_ref.at[:, cols(me.zh, y)], got.at[1, slot], me.at(y=y)) for slot, y in enumerate(me.ys())
    ]
    total = grad_ref[:, cols(1 - me.zh, me.y)].astype(F32)
    for slot, copy in enumerate(first):
        copy.wait_recv()
        total += got[0, slot].astype(F32)
    far_out[...] = total.astype(BF)
    crossing = copies.send(far_out, far_in, far)
    total = grad_ref[:, cols(me.zh, me.y)].astype(F32)
    for slot, copy in enumerate(second):
        copy.wait_recv()
        total += got[1, slot].astype(F32)
    for copy in inner_sent:
        copy.wait_recv()
    row = jnp.sum(inners[...], axis=0)
    lanes = lax.broadcasted_iota(jnp.int32, (128, 128), 0) == lax.broadcasted_iota(jnp.int32, (128, 128), 1)
    inner = jnp.concatenate(
        [
            jnp.sum(jnp.where(lanes, jnp.broadcast_to(row[k : k + 1], (128, 128)), 0.0), axis=1, keepdims=True)
            for k in range(frames // 128)
        ],
        axis=0,
    )
    factor = factor_ref[:, 0:1]
    scale = factor * factor * factor * inner * (1.0 / (8 * width))
    crossing.wait_recv()
    total += far_in[...].astype(F32)
    dpre = (factor * total - mine_ref[...].astype(F32) * scale).astype(BF)
    turned = dpre.astype(F32).T.astype(BF)

    def product(x):
        for zl in range(4):
            u = zl // 2
            value = jnp.dot(
                turned[u * 2 * block : (u + 1) * 2 * block],
                full_ref[:, columns((zl % 2) * 4 + x, width)],
                preferred_element_type=F32,
            ).astype(BF)
            gp[x, 0, zl] = value[block:]
            gp[x, 1, zl] = value[:block]
        return copies.send(gp.at[x, 1 - me.c], core_got.at[x], other)

    order = me.xs() + [me.x]
    in_core = [product(x) for x in order]
    along = []
    for slot, x in enumerate(order):
        in_core[slot].wait_recv()
        for zl in range(4):
            group[x, zl] = (gp[x, me.c, zl].astype(F32) + core_got[x, zl].astype(F32)).astype(BF)
        if slot < 3:
            along.append(copies.send(group.at[x], group_got.at[slot], me.at(x=x)))
    for copy in along:
        copy.wait_recv()
    for zl in range(4):
        value = group[me.x, zl].astype(F32)
        for slot in range(3):
            value += group_got[slot, zl].astype(F32)
        line[zl] = value.astype(BF)
    lines = [copies.send(line.at[zl], line_got.at[slot], me.at(zl=zl)) for slot, zl in enumerate(me.zls())]
    value = line[me.zl].astype(F32)
    for slot, copy in enumerate(lines):
        copy.wait_recv()
        value += line_got[slot].astype(F32)
    last[...] = value.astype(BF)
    home = copies.send(last, out_ref, me.to_owner())
    home.wait_recv()
    copies.finish()


def back(grad, inner, mine, factor, full, block):
    frames, width = mine.shape
    vmem = pl.BlockSpec(memory_space=pltpu.VMEM)
    return pl.pallas_call(
        back_kernel,
        out_shape=jax.ShapeDtypeStruct((block, width), BF),
        in_specs=[vmem] * 5,
        out_specs=vmem,
        scratch_shapes=[
            pltpu.VMEM((2, 3, frames, width), BF),
            pltpu.VMEM((frames, width), BF),
            pltpu.VMEM((frames, width), BF),
            pltpu.VMEM((8, 8, 128), F32),
            pltpu.VMEM((4, 2, 4, block, width), BF),
            pltpu.VMEM((4, 4, block, width), BF),
            pltpu.VMEM((4, 4, block, width), BF),
            pltpu.VMEM((3, 4, block, width), BF),
            pltpu.VMEM((4, block, width), BF),
            pltpu.VMEM((3, block, width), BF),
            pltpu.VMEM((block, width), BF),
            pltpu.SemaphoreType.DMA((32,)),
            pltpu.SemaphoreType.DMA((32,)),
        ],
        compiler_params=pltpu.CompilerParams(
            collective_id=3, has_side_effects=True, vmem_limit_bytes=VMEM_LIMIT
        ),
        name="back",
    )(grad, inner, mine, factor, full)


def inverse_rms(values):
    return lax.rsqrt(jnp.mean(values * values, axis=-1, keepdims=True) + EPSILON)


def previous_codes(codes):
    shifted = jnp.concatenate([jnp.zeros((1,), jnp.int32), codes[-1, :-1]])
    return jnp.concatenate([shifted[None, :], codes[:-1]], axis=0)


def local(attn_out, resid, out_proj, section_in, codebook, decays, section_out, codes):
    frame_count = attn_out.shape[0]
    depth_rank = lax.axis_index("depth")
    section_in, codebook, section_out = section_in[0], codebook[0], section_out[0]
    code_count, inner_width = codebook.shape
    pre, mine, section_full, attn_full, decs = front(attn_out, resid, out_proj, section_in, decays)
    section_full = section_full.reshape(-1, inner_width)

    factor = inverse_rms(pre.astype(F32))
    projected = jnp.dot(pre, section_full, preferred_element_type=F32)
    code_ids = lax.dynamic_index_in_dim(previous_codes(codes), depth_rank, 0, keepdims=False)
    positions = jnp.arange(frame_count, dtype=jnp.int32) % LENGTH
    keep_mask = jnp.logical_or(depth_rank != 0, positions != 0).astype(F32)[:, None]
    embedded = jnp.take(codebook, code_ids, axis=0).astype(F32) * keep_mask
    inputs = (projected * factor + embedded).astype(BF)

    states = scan(False, inputs, decs)

    normed = states.astype(F32) * inverse_rms(states.astype(F32))
    norm = inverse_rms(states.astype(F32))
    logits = jnp.dot(states, section_out, preferred_element_type=F32) * norm
    total_log = jax.nn.logsumexp(logits, axis=1)
    targets = lax.dynamic_index_in_dim(codes, depth_rank, 0, keepdims=False)
    chosen = jnp.arange(code_count, dtype=jnp.int32)[None, :] == targets[:, None]
    picked = jnp.sum(jnp.where(chosen, logits, 0.0), axis=1)
    losses = (total_log - picked)[None]
    dlogits = (jnp.exp(logits - total_log[:, None]) - chosen.astype(F32)).astype(BF)
    dnormed = lax.dot_general(dlogits, section_out, NT, preferred_element_type=F32)
    inner = jnp.sum(dlogits.astype(F32) * logits, axis=1, keepdims=True) / inner_width
    dstates = (norm * (dnormed - normed * inner)).astype(BF)

    carried = scan(True, dstates, decs)

    grad = lax.dot_general(carried, section_full, NT, preferred_element_type=F32).astype(BF)
    inner = jnp.sum(carried.astype(F32) * projected, axis=1).reshape(-1, 128)
    inner = jnp.pad(inner, ((0, 8 - inner.shape[0]), (0, 0)))
    grad_out = back(
        grad, inner, mine, jnp.broadcast_to(factor, (frame_count, 128)), attn_full, out_proj.shape[0]
    )
    return (losses, grad_out)


def solution(mesh):
    return jax.shard_map(
        local,
        mesh=mesh,
        in_specs=(
            P("wide", "depth"),
            P("wide", None),
            P("wide", "depth"),
            P("depth", "wide", None),
            P("depth", None, None),
            P("depth", None),
            P("depth", None, None),
            P(None, "wide"),
        ),
        out_specs=(P("depth", "wide"), P("wide", "depth")),
        check_vma=False,
    )
```

```python
import jax
import jax.numpy as jnp
from jax import lax
from jax.experimental import pallas as pl
from jax.experimental.pallas import tpu as pltpu
from jax.sharding import PartitionSpec as P

MESH = pl.DeviceIdType.MESH
LENGTH = 256
EPSILON = 1e-06
BF = jnp.bfloat16
F32 = jnp.float32
VMEM_LIMIT = 56 << 20
CHUNKS = 4
NT = (((1,), (1,)), ((), ()))


class Place:
    def __init__(self):
        w, d = lax.axis_index("wide"), lax.axis_index("depth")
        self.zl, self.x, self.c = w // 8, (w // 2) % 4, w % 2
        self.zh, self.y = d // 4, d % 4
        self.d = d

    def at(self, zl=None, x=None, c=None, zh=None, y=None):
        zl = self.zl if zl is None else zl
        x = self.x if x is None else x
        c = self.c if c is None else c
        zh = self.zh if zh is None else zh
        y = self.y if y is None else y
        return (zl * 8 + x * 2 + c, zh * 4 + y)

    def ys(self):
        return [(self.y + k) % 4 for k in (2, 1, 3)]

    def xs(self):
        return [(self.x + k) % 4 for k in (2, 1, 3)]

    def zls(self):
        return [(self.zl + k) % 4 for k in (2, 1, 3)]

    def to_features(self):
        return dict(
            zl=self.c * 2 + self.zh,
            x=self.y,
            c=1 - self.x % 2,
            zh=self.zl // 2,
            y=(self.zl % 2) * 2 + self.x // 2,
        )

    def to_owner(self):
        return dict(
            zl=self.zh * 2 + self.y // 2,
            x=(self.y % 2) * 2 + 1 - self.c,
            c=self.zl // 2,
            zh=self.zl % 2,
            y=self.x,
        )


class Copies:
    def __init__(self, send_sem, recv_sem):
        self.send_sem, self.recv_sem = send_sem, recv_sem
        self.used = 0
        self.sent = []

    def make(self, source, target, device):
        copy = pltpu.make_async_remote_copy(
            src_ref=source,
            dst_ref=target,
            send_sem=self.send_sem.at[self.used],
            recv_sem=self.recv_sem.at[self.used],
            device_id=device,
            device_id_type=MESH,
        )
        self.used += 1
        return copy

    def send(self, source, target, device):
        copy = self.make(source, target, device)
        copy.start()
        self.sent.append(copy)
        return copy

    def finish(self):
        for copy in self.sent:
            copy.wait_send()


def arrived(copies):
    for copy in copies:
        copy.wait_recv()


def greet(senders, targets):
    barrier = pltpu.get_barrier_semaphore()
    for device in senders:
        pl.semaphore_signal(barrier, inc=1, device_id=device, device_id_type=MESH)
    pl.semaphore_wait(barrier, len(targets))


def part(index, size):
    return pl.ds(pl.multiple_of(index * size, size), size)


def diagonal():
    return lax.broadcasted_iota(jnp.int32, (128, 128), 0) == lax.broadcasted_iota(jnp.int32, (128, 128), 1)


def to_column(row):
    eye = diagonal()
    pieces = [
        jnp.sum(
            jnp.where(eye, jnp.broadcast_to(row[:, k : k + 128], (128, 128)), 0.0), axis=1, keepdims=True
        )
        for k in range(0, row.shape[1], 128)
    ]
    return jnp.concatenate(pieces, axis=0)


def to_row(column):
    eye = diagonal()
    pieces = [
        jnp.sum(
            jnp.where(eye, jnp.broadcast_to(column[k : k + 128], (128, 128)), 0.0), axis=0, keepdims=True
        )
        for k in range(0, column.shape[0], 128)
    ]
    return jnp.concatenate(pieces, axis=1)


def kernel(
    attn_ref, resid_ref, proj_ref, sec_ref, book_ref, dec_ref, head_ref, codes_ref,
    loss_ref, out_ref,
    wd, resid_part, full, pre, mine, sect, decs, book, head, embed, proj_in, logits, dlogits,
    to_scan, got, done, states, carry_in, carry_out,
    gsend, ggot, far_out, far_in, inners, gp, core_got, group, group_got, line, line_got, last,
    send_sem, recv_sem, local_sem,
):
    me = Place()
    copies = Copies(send_sem, recv_sem)
    frames, width = attn_ref.shape
    block = proj_ref.shape[0]
    inner_width = sec_ref.shape[1]
    chunk = inner_width // CHUNKS
    code_count = book.shape[0]
    rows = frames // 4
    half_frames = frames // 2

    local = [
        pltpu.make_async_copy(resid_ref.at[:, part(me.d, width)], resid_part, local_sem.at[0]),
        pltpu.make_async_copy(book_ref, book, local_sem.at[1]),
        pltpu.make_async_copy(head_ref, head, local_sem.at[2]),
    ]
    for copy in local:
        copy.start()
    carry_in[...] = jnp.zeros_like(carry_in)
    decs[me.y] = jnp.broadcast_to(dec_ref[...], decs.shape[1:])
    for j in range(CHUNKS):
        sect[j, me.zl, me.x, me.c] = sec_ref[:, j * chunk : (j + 1) * chunk]
    full[:, part(me.d, width)] = attn_ref[...]

    y_peers = [me.at(y=y) for y in me.ys()]
    x_peers = [me.at(x=x) for x in me.xs()]
    zl_peers = [me.at(zl=zl) for zl in me.zls()]
    right, left = me.at(x=(me.x + 1) % 4), me.at(x=(me.x + 3) % 4)
    far, other = me.at(zh=1 - me.zh), me.at(c=1 - me.c)
    cross = [me.at(zh=1 - me.zh, y=y) for y in me.ys()]
    there, home = me.to_features(), me.to_owner()
    shared = y_peers + x_peers + zl_peers + cross + [far, other]
    both = shared + [me.at(**there), me.at(**home)]
    greet(both, both)

    def gather_depth(buffer, source):
        own = buffer.at[:, part(me.d, width)]
        halves = []
        for k in range(2):
            place = buffer.at[pl.ds(k * half_frames, half_frames), part(me.d, width)]
            halves.append(copies.send(source.at[pl.ds(k * half_frames, half_frames)], place, far))
        near = [copies.send(source, own, peer) for peer in y_peers]

        def onward():
            sent = []
            for k in range(2):
                halves[k].wait_recv()
                place = buffer.at[
                    pl.ds(k * half_frames, half_frames), part((1 - me.zh) * 4 + me.y, width)
                ]
                sent += [copies.send(place, place, peer) for peer in y_peers]
            return sent

        return near, onward

    class Ring:
        def __init__(self, slot, view):
            self.slot, self.view = slot, view
            self.cores = []

        def line(self):
            self.zs = [copies.send(self.slot, self.slot, peer) for peer in zl_peers]

        def first(self):
            arrived(self.zs)
            group = self.view(me.x)
            self.right = copies.send(group, group, right)
            self.left = copies.send(group, group, left)
            self.cores.append(copies.send(group, group, other))

        def second(self):
            self.right.wait_recv()
            x = (me.x + 3) % 4
            self.on_right = copies.send(self.view(x, 0), self.view(x, 0), right)
            self.cores.append(copies.send(self.view(x), self.view(x), other))
            self.left.wait_recv()
            x = (me.x + 1) % 4
            self.on_left = copies.send(self.view(x, 1), self.view(x, 1), left)
            self.cores.append(copies.send(self.view(x), self.view(x), other))

        def third(self):
            arrived([self.on_right, self.on_left])
            group = self.view((me.x + 2) % 4)
            self.cores.append(copies.send(group, group, other))

        def end(self):
            arrived(self.cores)

    def wd_view(x, half=None):
        return wd.at[me.c, x] if half is None else wd.at[me.c, x, half]

    def sect_view(j):
        def view(x, half=None):
            return sect.at[j, :, x, me.c] if half is None else sect.at[j, pl.ds(2 * half, 2), x, me.c]

        return view

    wd_ring = Ring(wd.at[me.c, me.x, me.zl % 2, me.zl // 2], wd_view)
    sec_rings = [Ring(sect.at[j, me.zl, me.x, me.c], sect_view(j)) for j in range(CHUNKS)]

    moved = copies.send(
        proj_ref, wd.at[there["c"], there["x"], there["zl"] % 2, there["zl"] // 2], me.at(**there)
    )
    attn_near, attn_onward = gather_depth(full, attn_ref)
    dec_near = [copies.send(decs.at[me.y], decs.at[me.y], peer) for peer in y_peers]
    sec_rings[0].line()
    moved.wait_recv()
    wd_ring.line()
    sec_rings[0].first()
    attn_near += attn_onward()
    sec_rings[0].second()
    wd_ring.first()
    sec_rings[1].line()

    codes = codes_ref[...].astype(F32)
    code_rows = lax.broadcasted_iota(jnp.int32, codes.shape, 0)
    lanes = lax.broadcasted_iota(jnp.int32, (1, frames), 1)
    target = to_column(jnp.sum(jnp.where(code_rows == me.d, codes, 0.0), axis=0, keepdims=True))
    before = jnp.sum(jnp.where(code_rows == me.d - 1, codes, 0.0), axis=0, keepdims=True)
    shifted = pltpu.roll(codes, 1, 1)[codes.shape[0] - 1 :]
    shifted = jnp.where(lanes % LENGTH == 0, -1.0, shifted)
    previous = to_column(jnp.where(me.d == 0, shifted, before))
    code_lanes = lax.broadcasted_iota(jnp.int32, (frames, code_count), 1).astype(F32)
    for copy in local:
        copy.wait()
    embed[...] = jnp.dot(
        jnp.where(code_lanes == previous, 1.0, 0.0).astype(BF), book[...], preferred_element_type=F32
    )

    wd_ring.second()
    sec_rings[1].first()
    sec_rings[2].line()
    sec_rings[0].third()
    wd_ring.third()
    wd_ring.end()
    arrived(attn_near)

    for u in range(2):
        total = jnp.zeros((frames, 2 * block), F32)
        for h in range(8):
            weight = wd[1 - u, h % 4, h // 4].reshape(2 * block, width)
            total += lax.dot_general(
                full[:, h * width : (h + 1) * width], weight, NT, preferred_element_type=F32
            )
        features = pl.ds(u * 2 * block, 2 * block)
        mine[:, features] = (resid_part[:, features].astype(F32) + total).astype(BF)
    pre[:, part(me.d, width)] = mine[...]
    pre_near, pre_onward = gather_depth(pre, mine)

    sec_rings[1].second()
    sec_rings[2].first()
    sec_rings[3].line()
    sec_rings[1].third()
    sec_rings[2].second()
    sec_rings[3].first()
    pre_far_near = pre_onward()
    sec_rings[2].third()
    sec_rings[3].second()

    def squares(zh):
        value = jnp.zeros((frames, 1), F32)
        for y in range(4):
            piece = pre[:, part(zh * 4 + y, width)].astype(F32)
            value += jnp.sum(piece * piece, axis=1, keepdims=True)
        return value

    arrived(pre_near)
    mean = squares(me.zh)
    sec_rings[3].third()
    arrived(pre_far_near + dec_near)
    mean += squares(1 - me.zh)
    factor = lax.rsqrt(mean * (1.0 / pre.shape[1]) + EPSILON)

    def exchange(backward, value):
        way = 1 if backward else 0
        first = 1 if backward else 0
        sent = []
        for j in range(CHUNKS):
            to_scan[way, j] = value(j).astype(BF)
            sent.append(
                [copies.send(to_scan.at[way, j, part(y, rows)], got.at[way, j, me.y], me.at(y=y)) for y in me.ys()]
            )
            got[way, j, me.y] = to_scan[way, j, part(me.y, rows)]
        returned, carries = [], []
        for j in range(CHUNKS):
            arrived(sent[j])
            carry = copies.make(carry_out.at[way, j], carry_in.at[way, j], far)
            carries.append(carry)

            @pl.when(me.zh != first)
            def _(carry=carry):
                carry.wait_recv()

            state = carry_in[way, j].astype(F32)
            for section in reversed(range(4)) if backward else range(4):
                decay = decs[section, 0:1, j * chunk : (j + 1) * chunk]
                if backward:
                    here = got[way, j, section].astype(F32) + state
                    done[way, j, section] = here.astype(BF)
                    state = decay * here
                else:
                    state = decay * state + got[way, j, section].astype(F32)
                    done[way, j, section] = state.astype(BF)
            carry_out[way, j] = state.astype(BF)

            @pl.when(me.zh == first)
            def _(carry=carry):
                carry.start()

            returned.append(
                [copies.send(done.at[way, j, y], states.at[way, j, part(me.y, rows)], me.at(y=y)) for y in me.ys()]
            )
            states[way, j, part(me.y, rows)] = done[way, j, me.y]
        return returned, carries, first

    def entering(j):
        sec_rings[j].end()
        value = jnp.dot(
            pre[...], sect[j].reshape(pre.shape[1], chunk), preferred_element_type=F32
        )
        proj_in[j] = value
        return value * factor + embed[:, j * chunk : (j + 1) * chunk]

    returned, carries, first = exchange(False, entering)

    mean = jnp.zeros((frames, 1), F32)
    for j in range(CHUNKS):
        arrived(returned[j])
        value = states[0, j]
        wide = value.astype(F32)
        mean += jnp.sum(wide * wide, axis=1, keepdims=True)
        term = jnp.dot(value, head[j * chunk : (j + 1) * chunk], preferred_element_type=F32)
        logits[...] = term if j == 0 else logits[...] + term
    norm = lax.rsqrt(mean * (1.0 / inner_width) + EPSILON)
    loss_parts, inner_parts = [], []
    step = 64
    for start in range(0, frames, step):
        piece = pl.ds(start, step)
        value = logits[piece] * norm[start : start + step]
        chosen = lax.broadcasted_iota(jnp.int32, (step, code_count), 1).astype(F32) == target[start : start + step]
        top = jnp.max(value, axis=1, keepdims=True)
        raised = jnp.exp(value - top)
        total = jnp.sum(raised, axis=1, keepdims=True)
        picked = jnp.sum(jnp.where(chosen, value, 0.0), axis=1, keepdims=True)
        loss_parts.append(top + jnp.log(total) - picked)
        slope = (raised * (1.0 / total) - jnp.where(chosen, 1.0, 0.0)).astype(BF)
        dlogits[piece] = slope
        inner_parts.append(jnp.sum(slope.astype(F32) * value, axis=1, keepdims=True))
    loss_ref[...] = to_row(jnp.concatenate(loss_parts, axis=0))
    inner = jnp.concatenate(inner_parts, axis=0) * (1.0 / inner_width)

    def leaving(j):
        value = lax.dot_general(
            dlogits[...], head[j * chunk : (j + 1) * chunk], NT, preferred_element_type=F32
        )
        return norm * (value - states[0, j].astype(F32) * (norm * inner))

    returned, more, last_first = exchange(True, leaving)

    inner = jnp.zeros((frames, 1), F32)
    for j in range(CHUNKS):
        arrived(returned[j])
        inner += jnp.sum(states[1, j].astype(F32) * proj_in[j], axis=1, keepdims=True)
    inners[me.d] = jnp.broadcast_to(to_row(inner), inners.shape[1:])

    def term(u, zh, y):
        d = zh * 4 + y
        total = jnp.zeros((frames, 2 * block), F32)
        for j in range(CHUNKS):
            weight = sect[j, d // 2, (d % 2) * 2 + u].reshape(2 * block, chunk)
            total += lax.dot_general(states[1, j], weight, NT, preferred_element_type=F32)
        return total

    sums, kept = [], []
    for u in range(2):
        for k, zh in enumerate((1 - me.zh, me.zh)):
            sent = []
            for slot, y in enumerate(me.ys()):
                gsend[u, k, slot] = term(u, zh, y).astype(BF)
                sent.append(copies.send(gsend.at[u, k, slot], ggot.at[u, k, slot], me.at(y=y)))
            sums.append(sent)
            kept.append(term(u, zh, me.y))
        if u == 0:
            inner_sent = [copies.send(inners.at[me.d], inners.at[me.d], peer) for peer in y_peers + [far] + cross]

    order = me.xs() + [me.x]
    line_order = me.zls() + [me.zl]
    along = [
        [copies.make(group.at[x, zl], group_got.at[slot, k], me.at(x=x)) for k, zl in enumerate(line_order)]
        for slot, x in enumerate(order[:3])
    ]
    in_core = [[copies.make(gp.at[u, x], core_got.at[x], other) for x in order] for u in range(2)]
    crossing = []
    for u in range(2):
        total = kept[2 * u]
        for slot, copy in enumerate(sums[2 * u]):
            copy.wait_recv()
            total += ggot[u, 0, slot].astype(F32)
        far_out[u] = total.astype(BF)
        crossing.append(copies.send(far_out.at[u], far_in.at[u], far))
        total = kept[2 * u + 1]
        for slot, copy in enumerate(sums[2 * u + 1]):
            copy.wait_recv()
            total += ggot[u, 1, slot].astype(F32)
        if u == 0:
            arrived(inner_sent)
            inner = to_column(jnp.sum(inners[...], axis=0)[0:1])
            scale = factor * factor * factor * inner * (1.0 / pre.shape[1])
        crossing[u].wait_recv()
        total += far_in[u].astype(F32)
        dpre = factor * total - mine[:, u * 2 * block : (u + 1) * 2 * block].astype(F32) * scale
        turned = dpre.T.astype(BF)

        for slot, x in enumerate(order):
            for zh in range(2):
                value = jnp.dot(turned, full[:, part(zh * 4 + x, width)], preferred_element_type=F32).astype(BF)
                gp[u, x, zh] = value[:block]
                gp[u, x, 2 + zh] = value[block:]

            @pl.when(me.c == u)
            def _(copy=in_core[u][slot]):
                copy.start()

        @pl.when(me.c != u)
        def _(u=u):
            for slot, x in enumerate(order):
                in_core[u][slot].wait_recv()
                for k, zl in enumerate(line_order):
                    group[x, zl] = (gp[u, x, zl].astype(F32) + core_got[x, zl].astype(F32)).astype(BF)
                    if slot < 3:
                        along[slot][k].start()

    lines = []
    for k, zl in enumerate(line_order):
        value = group[me.x, zl].astype(F32)
        for slot in range(3):
            along[slot][k].wait_recv()
            value += group_got[slot, k].astype(F32)
        if k < 3:
            line[k] = value.astype(BF)
            lines.append(copies.send(line.at[k], line_got.at[k], me.at(zl=zl)))
    for k, copy in enumerate(lines):
        copy.wait_recv()
        value += line_got[k].astype(F32)
    last[...] = value.astype(BF)
    ending = copies.send(last, out_ref, me.at(**home))
    for u in range(2):

        @pl.when(me.c == u)
        def _(u=u):
            for copy in in_core[u]:
                copy.wait_send()

    for copies_of_slot in along:
        for copy in copies_of_slot:
            copy.wait_send()
    for made, start_at in ((carries, first), (more, last_first)):

        @pl.when(me.zh == start_at)
        def _(made=made):
            for copy in made:
                copy.wait_send()

    copies.finish()
    ending.wait_recv()


def local(attn_out, resid, out_proj, section_in, codebook, decays, section_out, codes):
    frames, width = attn_out.shape
    block = out_proj.shape[0]
    _, rows_in, inner = section_in.shape
    code_count = codebook.shape[1]
    chunk = inner // CHUNKS
    rows = frames // 4
    vmem = pl.BlockSpec(memory_space=pltpu.VMEM)
    anywhere = pl.BlockSpec(memory_space=pl.ANY)
    copies = 224
    return pl.pallas_call(
        kernel,
        out_shape=(
            jax.ShapeDtypeStruct((1, frames), F32),
            jax.ShapeDtypeStruct((block, width), BF),
        ),
        in_specs=[vmem, anywhere, vmem, vmem, anywhere, vmem, anywhere, vmem],
        out_specs=[vmem, vmem],
        scratch_shapes=[
            pltpu.VMEM((2, 4, 2, 2, block, width), BF),
            pltpu.VMEM((frames, width), BF),
            pltpu.VMEM((frames, 8 * width), BF),
            pltpu.VMEM((frames, 8 * width), BF),
            pltpu.VMEM((frames, width), BF),
            pltpu.VMEM((CHUNKS, 4, 4, 2, rows_in, chunk), BF),
            pltpu.VMEM((4, 8, inner), F32),
            pltpu.VMEM((code_count, inner), BF),
            pltpu.VMEM((inner, code_count), BF),
            pltpu.VMEM((frames, inner), F32),
            pltpu.VMEM((CHUNKS, frames, chunk), F32),
            pltpu.VMEM((frames, code_count), F32),
            pltpu.VMEM((frames, code_count), BF),
            pltpu.VMEM((2, CHUNKS, frames, chunk), BF),
            pltpu.VMEM((2, CHUNKS, 4, rows, chunk), BF),
            pltpu.VMEM((2, CHUNKS, 4, rows, chunk), BF),
            pltpu.VMEM((2, CHUNKS, frames, chunk), BF),
            pltpu.VMEM((2, CHUNKS, rows, chunk), BF),
            pltpu.VMEM((2, CHUNKS, rows, chunk), BF),
            pltpu.VMEM((2, 2, 3, frames, 2 * block), BF),
            pltpu.VMEM((2, 2, 3, frames, 2 * block), BF),
            pltpu.VMEM((2, frames, 2 * block), BF),
            pltpu.VMEM((2, frames, 2 * block), BF),
            pltpu.VMEM((8, 8, frames), F32),
            pltpu.VMEM((2, 4, 4, block, width), BF),
            pltpu.VMEM((4, 4, block, width), BF),
            pltpu.VMEM((4, 4, block, width), BF),
            pltpu.VMEM((3, 4, block, width), BF),
            pltpu.VMEM((3, block, width), BF),
            pltpu.VMEM((3, block, width), BF),
            pltpu.VMEM((block, width), BF),
            pltpu.SemaphoreType.DMA((copies,)),
            pltpu.SemaphoreType.DMA((copies,)),
            pltpu.SemaphoreType.DMA((3,)),
        ],
        compiler_params=pltpu.CompilerParams(
            collective_id=0, has_side_effects=True, vmem_limit_bytes=VMEM_LIMIT
        ),
        name="whole",
    )(attn_out, resid, out_proj, section_in[0], codebook[0], decays, section_out[0], codes)


def solution(mesh):
    return jax.shard_map(
        local,
        mesh=mesh,
        in_specs=(
            P("wide", "depth"),
            P("wide", None),
            P("wide", "depth"),
            P("depth", "wide", None),
            P("depth", None, None),
            P("depth", None),
            P("depth", None, None),
            P(None, "wide"),
        ),
        out_specs=(P("depth", "wide"), P("wide", "depth")),
        check_vma=False,
    )
```

```python
import jax
import jax.numpy as jnp
from jax import lax
from jax.experimental import pallas as pl
from jax.experimental.pallas import tpu as pltpu
from jax.sharding import PartitionSpec as P

MESH = pl.DeviceIdType.MESH
LENGTH = 256
EPSILON = 1e-06
BF = jnp.bfloat16
F32 = jnp.float32
VMEM_LIMIT = 56 << 20
CHUNKS = 4
NT = (((1,), (1,)), ((), ()))


class Place:
    def __init__(self):
        w, d = lax.axis_index("wide"), lax.axis_index("depth")
        self.zl, self.x, self.c = w // 8, (w // 2) % 4, w % 2
        self.zh, self.y = d // 4, d % 4
        self.d = d

    def at(self, zl=None, x=None, c=None, zh=None, y=None):
        zl = self.zl if zl is None else zl
        x = self.x if x is None else x
        c = self.c if c is None else c
        zh = self.zh if zh is None else zh
        y = self.y if y is None else y
        return (zl * 8 + x * 2 + c, zh * 4 + y)

    def ys(self):
        return [(self.y + k) % 4 for k in (2, 1, 3)]

    def xs(self):
        return [(self.x + k) % 4 for k in (2, 1, 3)]

    def zls(self):
        return [(self.zl + k) % 4 for k in (2, 1, 3)]

    def to_features(self):
        return dict(
            zl=(self.x % 2) * 2 + self.zh,
            x=self.y,
            c=1 - self.c,
            zh=self.zl // 2,
            y=(self.zl % 2) * 2 + self.x // 2,
        )

    def to_owner(self):
        return dict(
            zl=self.zh * 2 + self.y // 2,
            x=(self.y % 2) * 2 + self.zl // 2,
            c=1 - self.c,
            zh=self.zl % 2,
            y=self.x,
        )


class Copies:
    def __init__(self, send_sem, recv_sem):
        self.send_sem, self.recv_sem = send_sem, recv_sem
        self.used = 0
        self.sent = []

    def make(self, source, target, device):
        copy = pltpu.make_async_remote_copy(
            src_ref=source,
            dst_ref=target,
            send_sem=self.send_sem.at[self.used],
            recv_sem=self.recv_sem.at[self.used],
            device_id=device,
            device_id_type=MESH,
        )
        self.used += 1
        return copy

    def send(self, source, target, device):
        copy = self.make(source, target, device)
        copy.start()
        self.sent.append(copy)
        return copy

    def finish(self):
        for copy in self.sent:
            copy.wait_send()


def arrived(copies):
    for copy in copies:
        copy.wait_recv()


def greet(senders, targets):
    barrier = pltpu.get_barrier_semaphore()
    for device in senders:
        pl.semaphore_signal(barrier, inc=1, device_id=device, device_id_type=MESH)
    pl.semaphore_wait(barrier, len(targets))


def part(index, size):
    return pl.ds(pl.multiple_of(index * size, size), size)


def diagonal():
    return lax.broadcasted_iota(jnp.int32, (128, 128), 0) == lax.broadcasted_iota(jnp.int32, (128, 128), 1)


def to_column(row):
    eye = diagonal()
    pieces = [
        jnp.sum(
            jnp.where(eye, jnp.broadcast_to(row[:, k : k + 128], (128, 128)), 0.0), axis=1, keepdims=True
        )
        for k in range(0, row.shape[1], 128)
    ]
    return jnp.concatenate(pieces, axis=0)


def to_row(column):
    eye = diagonal()
    pieces = [
        jnp.sum(
            jnp.where(eye, jnp.broadcast_to(column[k : k + 128], (128, 128)), 0.0), axis=0, keepdims=True
        )
        for k in range(0, column.shape[0], 128)
    ]
    return jnp.concatenate(pieces, axis=1)


def kernel(
    attn_ref, resid_ref, proj_ref, sec_ref, book_ref, dec_ref, head_ref, codes_ref,
    loss_ref, out_ref,
    turned, wd, resid_part, full, pre, mine, sect, decs, book, head, embed, proj_in, logits, dlogits,
    to_scan, got, done, states, carry_in, carry_out,
    gsend, ggot, far_out, far_in, inners, gp, core_got, group, group_got, line, line_got, last,
    send_sem, recv_sem, local_sem, line_send, line_recv,
):
    me = Place()
    copies = Copies(send_sem, recv_sem)
    frames, width = attn_ref.shape
    block = proj_ref.shape[0]
    inner_width = sec_ref.shape[1]
    chunk = inner_width // CHUNKS
    code_count = book.shape[0]
    rows = frames // 4
    half_frames = frames // 2

    local = [
        pltpu.make_async_copy(resid_ref.at[:, part(me.d, width)], resid_part, local_sem.at[0]),
        pltpu.make_async_copy(book_ref, book, local_sem.at[1]),
        pltpu.make_async_copy(head_ref, head, local_sem.at[2]),
    ]
    for copy in local:
        copy.start()
    carry_in[...] = jnp.zeros_like(carry_in)
    decs[me.y] = jnp.broadcast_to(dec_ref[...], decs.shape[1:])
    for j in range(CHUNKS):
        sect[j, me.zl, me.x, me.c] = sec_ref[:, j * chunk : (j + 1) * chunk]
    full[:, part(me.d, width)] = attn_ref[...]

    y_peers = [me.at(y=y) for y in me.ys()]
    x_peers = [me.at(x=x) for x in me.xs()]
    zl_peers = [me.at(zl=zl) for zl in me.zls()]
    right, left = me.at(x=(me.x + 1) % 4), me.at(x=(me.x + 3) % 4)
    far, other = me.at(zh=1 - me.zh), me.at(c=1 - me.c)
    cross = [me.at(zh=1 - me.zh, y=y) for y in me.ys()]
    there, home = me.to_features(), me.to_owner()
    shared = y_peers + x_peers + zl_peers + cross + [far, other]
    both = shared + [me.at(**there), me.at(**home)]
    greet(both, both)

    def gather_depth(buffer, source):
        halves = []
        for k in range(2):
            place = buffer.at[pl.ds(k * half_frames, half_frames), part(me.d, width)]
            halves.append(copies.send(source.at[pl.ds(k * half_frames, half_frames)], place, far))

        def onward(k):
            halves[k].wait_recv()
            place = buffer.at[pl.ds(k * half_frames, half_frames), part((1 - me.zh) * 4 + me.y, width)]
            return [copies.send(place, place, peer) for peer in y_peers]

        return onward

    def gather_near(buffer, source):
        own = buffer.at[:, part(me.d, width)]
        return [copies.send(source, own, peer) for peer in y_peers]

    class Ring:
        def __init__(self, slot, view):
            self.slot, self.view = slot, view
            self.cores = []

        def line(self):
            self.zs = [copies.send(self.slot, self.slot, peer) for peer in zl_peers]

        def first(self):
            arrived(self.zs)
            group = self.view(me.x)
            self.right = copies.send(group, group, right)
            self.left = copies.send(group, group, left)
            self.cores.append(copies.send(group, group, other))

        def second(self):
            self.right.wait_recv()
            x = (me.x + 3) % 4
            self.on_right = copies.send(self.view(x, 0), self.view(x, 0), right)
            self.cores.append(copies.send(self.view(x), self.view(x), other))
            self.left.wait_recv()
            x = (me.x + 1) % 4
            self.on_left = copies.send(self.view(x, 1), self.view(x, 1), left)
            self.cores.append(copies.send(self.view(x), self.view(x), other))

        def third(self):
            arrived([self.on_right, self.on_left])
            group = self.view((me.x + 2) % 4)
            self.cores.append(copies.send(group, group, other))

        def end(self):
            arrived(self.cores)

    half_block = block // 2

    def wd_view(k):
        lines = pl.ds(k * half_block, half_block)

        def view(x, half=None):
            zls = slice(None) if half is None else pl.ds(2 * half, 2)
            return wd.at[zls, x, 1 - me.c, lines]

        return view

    def sect_view(j):
        def view(x, half=None):
            return sect.at[j, :, x, me.c] if half is None else sect.at[j, pl.ds(2 * half, 2), x, me.c]

        return view

    wd_rings = [
        Ring(wd.at[me.zl, me.x, 1 - me.c, pl.ds(k * half_block, half_block)], wd_view(k))
        for k in range(2)
    ]
    sec_rings = [Ring(sect.at[j, me.zl, me.x, me.c], sect_view(j)) for j in range(CHUNKS)]

    moved = copies.send(
        proj_ref, wd.at[there["zl"], there["x"], 1 - there["c"]], me.at(**there)
    )
    sec_rings[0].line()
    moved.wait_recv()
    for ring in wd_rings:
        ring.line()
    attn_near = gather_near(full, attn_ref)
    dec_near = [copies.send(decs.at[me.y], decs.at[me.y], peer) for peer in y_peers]
    sec_rings[0].first()
    wd_rings[0].first()
    attn_onward = gather_depth(full, attn_ref)
    sec_rings[0].second()
    wd_rings[1].first()

    codes = codes_ref[...].astype(F32)
    code_rows = lax.broadcasted_iota(jnp.int32, codes.shape, 0)
    lanes = lax.broadcasted_iota(jnp.int32, (1, frames), 1)
    target = to_column(jnp.sum(jnp.where(code_rows == me.d, codes, 0.0), axis=0, keepdims=True))
    before = jnp.sum(jnp.where(code_rows == me.d - 1, codes, 0.0), axis=0, keepdims=True)
    shifted = pltpu.roll(codes, 1, 1)[codes.shape[0] - 1 :]
    shifted = jnp.where(lanes % LENGTH == 0, -1.0, shifted)
    previous = to_column(jnp.where(me.d == 0, shifted, before))
    code_lanes = lax.broadcasted_iota(jnp.int32, (frames, code_count), 1).astype(F32)
    for copy in local:
        copy.wait()
    embed[...] = jnp.dot(
        jnp.where(code_lanes == previous, 1.0, 0.0).astype(BF), book[...], preferred_element_type=F32
    )

    sec_rings[1].line()
    wd_rings[0].second()
    attn_near += attn_onward(0)
    wd_rings[1].second()
    attn_near += attn_onward(1)
    sec_rings[2].line()
    sec_rings[0].third()
    sec_rings[1].first()
    wd_rings[0].third()
    wd_rings[1].third()
    for ring in wd_rings:
        ring.end()
    arrived(attn_near)

    for u in range(2):
        total = jnp.zeros((frames, 2 * block), F32)
        for h in range(8):
            weight = wd[2 * u + h // 4, h % 4].reshape(2 * block, width)
            total += lax.dot_general(
                full[:, h * width : (h + 1) * width], weight, NT, preferred_element_type=F32
            )
        features = pl.ds(u * 2 * block, 2 * block)
        mine[:, features] = (resid_part[:, features].astype(F32) + total).astype(BF)
    pre[:, part(me.d, width)] = mine[...]
    pre_onward = gather_depth(pre, mine)
    pre_near = gather_near(pre, mine)

    def squares(zh):
        value = pre[:, part(zh, 4 * width)].astype(F32)
        return jnp.sum(value * value, axis=1, keepdims=True)

    def projection(j, zh):
        weight = sect[j, pl.ds(2 * zh, 2)].reshape(4 * width, chunk)
        return jnp.dot(pre[:, part(zh, 4 * width)], weight, preferred_element_type=F32)

    sec_rings[1].second()
    sec_rings[2].first()
    sec_rings[3].line()
    pre_far_near = pre_onward(0)
    sec_rings[1].third()
    sec_rings[2].second()
    pre_far_near += pre_onward(1)
    sec_rings[3].first()
    arrived(pre_near)
    mean = squares(me.zh)
    for j in range(2):
        sec_rings[j].end()
        proj_in[j] = projection(j, me.zh)
    sec_rings[2].third()
    sec_rings[3].second()
    arrived(pre_far_near + dec_near)
    mean += squares(1 - me.zh)
    factor = lax.rsqrt(mean * (1.0 / pre.shape[1]) + EPSILON)

    def exchange(backward, value):
        way = 1 if backward else 0
        first = 1 if backward else 0
        sent = []
        for j in range(CHUNKS):
            to_scan[way, j] = value(j).astype(BF)
            sent.append(
                [copies.send(to_scan.at[way, j, part(y, rows)], got.at[way, j, me.y], me.at(y=y)) for y in me.ys()]
            )
            got[way, j, me.y] = to_scan[way, j, part(me.y, rows)]
        returned, carries = [], []
        for j in range(CHUNKS):
            arrived(sent[j])
            carry = copies.make(carry_out.at[way, j], carry_in.at[way, j], far)
            carries.append(carry)

            @pl.when(me.zh != first)
            def _(carry=carry):
                carry.wait_recv()

            state = carry_in[way, j].astype(F32)
            for section in reversed(range(4)) if backward else range(4):
                decay = decs[section, 0:1, j * chunk : (j + 1) * chunk]
                if backward:
                    here = got[way, j, section].astype(F32) + state
                    done[way, j, section] = here.astype(BF)
                    state = decay * here
                else:
                    state = decay * state + got[way, j, section].astype(F32)
                    done[way, j, section] = state.astype(BF)
            carry_out[way, j] = state.astype(BF)

            @pl.when(me.zh == first)
            def _(carry=carry):
                carry.start()

            returned.append(
                [copies.send(done.at[way, j, y], states.at[way, j, part(me.y, rows)], me.at(y=y)) for y in me.ys()]
            )
            states[way, j, part(me.y, rows)] = done[way, j, me.y]
        return returned, carries, first

    def entering(j):
        if j == 3:
            sec_rings[3].third()
        if j >= 2:
            sec_rings[j].end()
            proj_in[j] = projection(j, me.zh)
        value = proj_in[j] + projection(j, 1 - me.zh)
        proj_in[j] = value
        return value * factor + embed[:, j * chunk : (j + 1) * chunk]

    returned, carries, first = exchange(False, entering)

    mean = jnp.zeros((frames, 1), F32)
    for j in range(CHUNKS):
        arrived(returned[j])
        value = states[0, j]
        wide = value.astype(F32)
        mean += jnp.sum(wide * wide, axis=1, keepdims=True)
        term = jnp.dot(value, head[j * chunk : (j + 1) * chunk], preferred_element_type=F32)
        logits[...] = term if j == 0 else logits[...] + term
    norm = lax.rsqrt(mean * (1.0 / inner_width) + EPSILON)
    loss_parts, inner_parts = [], []
    step = 64
    for start in range(0, frames, step):
        piece = pl.ds(start, step)
        value = logits[piece] * norm[start : start + step]
        chosen = lax.broadcasted_iota(jnp.int32, (step, code_count), 1).astype(F32) == target[start : start + step]
        top = jnp.max(value, axis=1, keepdims=True)
        raised = jnp.exp(value - top)
        total = jnp.sum(raised, axis=1, keepdims=True)
        picked = jnp.sum(jnp.where(chosen, value, 0.0), axis=1, keepdims=True)
        loss_parts.append(top + jnp.log(total) - picked)
        slope = (raised * (1.0 / total) - jnp.where(chosen, 1.0, 0.0)).astype(BF)
        dlogits[piece] = slope
        inner_parts.append(jnp.sum(slope.astype(F32) * value, axis=1, keepdims=True))
    loss_ref[...] = to_row(jnp.concatenate(loss_parts, axis=0))
    inner = jnp.concatenate(inner_parts, axis=0) * (1.0 / inner_width)

    def leaving(j):
        value = lax.dot_general(
            dlogits[...], head[j * chunk : (j + 1) * chunk], NT, preferred_element_type=F32
        )
        return norm * (value - states[0, j].astype(F32) * (norm * inner))

    returned, more, last_first = exchange(True, leaving)

    inner = jnp.zeros((frames, 1), F32)
    for j in range(CHUNKS):
        arrived(returned[j])
        inner += jnp.sum(states[1, j].astype(F32) * proj_in[j], axis=1, keepdims=True)
    inners[me.d] = jnp.broadcast_to(to_row(inner), inners.shape[1:])
    inner_sent = [copies.send(inners.at[me.d], inners.at[me.d], peer) for peer in y_peers + [far] + cross]

    def term(u, zh, y):
        d = zh * 4 + y
        total = jnp.zeros((frames, 2 * block), F32)
        for j in range(CHUNKS):
            weight = sect[j, d // 2, (d % 2) * 2 + u].reshape(2 * block, chunk)
            total += lax.dot_general(states[1, j], weight, NT, preferred_element_type=F32)
        return total

    sums, kept = {}, {}
    order = me.xs() + [me.x]
    for u in range(2):
        for k, zh in enumerate((1 - me.zh, me.zh)):
            for slot, y in enumerate(me.ys()):
                value = term(u, zh, y).astype(BF)
                for lo in range(2):
                    gsend[2 * u + lo, k, slot] = value[:, lo * block : (lo + 1) * block]
            kept[u, k] = term(u, zh, me.y)
            sums[2 * u, k] = [
                copies.send(gsend.at[2 * u, k, slot], ggot.at[2 * u, k, slot], me.at(y=y))
                for slot, y in enumerate(me.ys())
            ]
        for k in range(2):
            sums[2 * u + 1, k] = [
                copies.send(gsend.at[2 * u + 1, k, slot], ggot.at[2 * u + 1, k, slot], me.at(y=y))
                for slot, y in enumerate(me.ys())
            ]

    along = [
        [
            [copies.make(group.at[hi, x, zh], group_got.at[slot, hi, zh], me.at(x=x)) for zh in range(2)]
            for slot, x in enumerate(order[:3])
        ]
        for hi in range(2)
    ]
    in_core = [[copies.make(gp.at[q, x], core_got.at[q // 2, x], other) for x in order] for q in range(4)]

    def reduced(q, k):
        lo = q % 2
        total = kept[q // 2, k][:, lo * block : (lo + 1) * block]
        for slot, copy in enumerate(sums[q, k]):
            copy.wait_recv()
            total += ggot[q, k, slot].astype(F32)
        return total

    def cross_part(q):
        far_out[q] = reduced(q, 0).astype(BF)
        return copies.send(far_out.at[q], far_in.at[q], far)

    crossing = [cross_part(0)]
    for q in range(4):
        total = reduced(q, 1)
        if q < 3:
            crossing.append(cross_part(q + 1))
        if q == 0:
            arrived(inner_sent)
            inner = to_column(jnp.sum(inners[...], axis=0)[0:1])
            scale = factor * factor * factor * inner * (1.0 / pre.shape[1])
        crossing[q].wait_recv()
        total += far_in[q].astype(F32)
        dpre = factor * total - mine[:, q * block : (q + 1) * block].astype(F32) * scale
        turned[q] = dpre.T.astype(BF)

        for slot, x in enumerate(order):
            for zh in range(2):
                gp[q, x, zh] = jnp.dot(
                    turned[q], full[:, part(zh * 4 + x, width)], preferred_element_type=F32
                ).astype(BF)

            @pl.when(me.c == q % 2)
            def _(copy=in_core[q][slot]):
                copy.start()

        @pl.when(me.c != q % 2)
        def _(q=q, hi=q // 2):
            for slot, x in enumerate(order):
                in_core[q][slot].wait_recv()
                for zh in range(2):
                    group[hi, x, zh] = (gp[q, x, zh].astype(F32) + core_got[hi, x, zh].astype(F32)).astype(BF)
                    if slot < 3:
                        along[hi][slot][zh].start()

    def line_copy(zl):
        return pltpu.make_async_remote_copy(
            src_ref=line.at[zl],
            dst_ref=line_got.at[me.zl],
            send_sem=line_send.at[zl],
            recv_sem=line_recv.at[me.zl],
            device_id=me.at(zl=zl),
            device_id_type=MESH,
        )

    for zl in range(4):
        hi, zh = zl // 2, zl % 2
        value = group[hi, me.x, zh].astype(F32)
        for slot in range(3):
            along[hi][slot][zh].wait_recv()
            value += group_got[slot, hi, zh].astype(F32)
        line[zl] = value.astype(BF)

        @pl.when(me.zl != zl)
        def _(zl=zl):
            line_copy(zl).start()

    value = line[me.zl].astype(F32)
    for k in range(1, 4):
        zl = (me.zl + k) % 4
        pltpu.make_async_remote_copy(
            src_ref=line.at[zl],
            dst_ref=line_got.at[zl],
            send_sem=line_send.at[zl],
            recv_sem=line_recv.at[zl],
            device_id=me.at(zl=zl),
            device_id_type=MESH,
        ).wait_recv()
        value += line_got[zl].astype(F32)
    last[...] = value.astype(BF)
    ending = copies.send(last, out_ref, me.at(**home))
    for zl in range(4):

        @pl.when(me.zl != zl)
        def _(zl=zl):
            line_copy(zl).wait_send()

    for q in range(4):

        @pl.when(me.c == q % 2)
        def _(q=q):
            for copy in in_core[q]:
                copy.wait_send()

    for side in along:
        for slot in side:
            for copy in slot:
                copy.wait_send()
    for made, start_at in ((carries, first), (more, last_first)):

        @pl.when(me.zh == start_at)
        def _(made=made):
            for copy in made:
                copy.wait_send()

    copies.finish()
    ending.wait_recv()


def local(attn_out, resid, out_proj, section_in, codebook, decays, section_out, codes):
    frames, width = attn_out.shape
    block = out_proj.shape[0]
    _, rows_in, inner = section_in.shape
    code_count = codebook.shape[1]
    chunk = inner // CHUNKS
    rows = frames // 4
    vmem = pl.BlockSpec(memory_space=pltpu.VMEM)
    anywhere = pl.BlockSpec(memory_space=pl.ANY)
    copies = 256
    return pl.pallas_call(
        kernel,
        out_shape=(
            jax.ShapeDtypeStruct((1, frames), F32),
            jax.ShapeDtypeStruct((block, width), BF),
        ),
        in_specs=[vmem, anywhere, vmem, vmem, anywhere, vmem, anywhere, vmem],
        out_specs=[vmem, vmem],
        scratch_shapes=[
            pltpu.VMEM((4, block, frames), BF),
            pltpu.VMEM((4, 4, 2, block, width), BF),
            pltpu.VMEM((frames, width), BF),
            pltpu.VMEM((frames, 8 * width), BF),
            pltpu.VMEM((frames, 8 * width), BF),
            pltpu.VMEM((frames, width), BF),
            pltpu.VMEM((CHUNKS, 4, 4, 2, rows_in, chunk), BF),
            pltpu.VMEM((4, 8, inner), F32),
            pltpu.VMEM((code_count, inner), BF),
            pltpu.VMEM((inner, code_count), BF),
            pltpu.VMEM((frames, inner), F32),
            pltpu.VMEM((CHUNKS, frames, chunk), F32),
            pltpu.VMEM((frames, code_count), F32),
            pltpu.VMEM((frames, code_count), BF),
            pltpu.VMEM((2, CHUNKS, frames, chunk), BF),
            pltpu.VMEM((2, CHUNKS, 4, rows, chunk), BF),
            pltpu.VMEM((2, CHUNKS, 4, rows, chunk), BF),
            pltpu.VMEM((2, CHUNKS, frames, chunk), BF),
            pltpu.VMEM((2, CHUNKS, rows, chunk), BF),
            pltpu.VMEM((2, CHUNKS, rows, chunk), BF),
            pltpu.VMEM((4, 2, 3, frames, block), BF),
            pltpu.VMEM((4, 2, 3, frames, block), BF),
            pltpu.VMEM((4, frames, block), BF),
            pltpu.VMEM((4, frames, block), BF),
            pltpu.VMEM((8, 8, frames), F32),
            pltpu.VMEM((4, 4, 2, block, width), BF),
            pltpu.VMEM((2, 4, 2, block, width), BF),
            pltpu.VMEM((2, 4, 2, block, width), BF),
            pltpu.VMEM((3, 2, 2, block, width), BF),
            pltpu.VMEM((4, block, width), BF),
            pltpu.VMEM((4, block, width), BF),
            pltpu.VMEM((block, width), BF),
            pltpu.SemaphoreType.DMA((copies,)),
            pltpu.SemaphoreType.DMA((copies,)),
            pltpu.SemaphoreType.DMA((3,)),
            pltpu.SemaphoreType.DMA((4,)),
            pltpu.SemaphoreType.DMA((4,)),
        ],
        compiler_params=pltpu.CompilerParams(
            collective_id=0, has_side_effects=True, vmem_limit_bytes=VMEM_LIMIT
        ),
        name="whole",
    )(attn_out, resid, out_proj, section_in[0], codebook[0], decays, section_out[0], codes)


def solution(mesh):
    return jax.shard_map(
        local,
        mesh=mesh,
        in_specs=(
            P("wide", "depth"),
            P("wide", None),
            P("wide", "depth"),
            P("depth", "wide", None),
            P("depth", None, None),
            P("depth", None),
            P("depth", None, None),
            P(None, "wide"),
        ),
        out_specs=(P("depth", "wide"), P("wide", "depth")),
        check_vma=False,
    )
```

```python
import jax
import jax.numpy as jnp
from jax import lax
from jax.experimental import pallas as pl
from jax.experimental.pallas import tpu as pltpu
from jax.sharding import PartitionSpec as P

MESH = pl.DeviceIdType.MESH
LENGTH = 256
EPSILON = 1e-06
BF = jnp.bfloat16
F32 = jnp.float32
VMEM_LIMIT = 56 << 20
CHUNKS = 4
PAIRS = ((0, 3), (1, 2))
NT = (((1,), (1,)), ((), ()))


class Place:
    def __init__(self):
        w, d = lax.axis_index("wide"), lax.axis_index("depth")
        self.zl, self.x, self.c = w // 8, (w // 2) % 4, w % 2
        self.zh, self.y = d // 4, d % 4
        self.d = d

    def at(self, zl=None, x=None, c=None, zh=None, y=None):
        zl = self.zl if zl is None else zl
        x = self.x if x is None else x
        c = self.c if c is None else c
        zh = self.zh if zh is None else zh
        y = self.y if y is None else y
        return (zl * 8 + x * 2 + c, zh * 4 + y)

    def ys(self):
        return [(self.y + k) % 4 for k in (2, 1, 3)]

    def xs(self):
        return [(self.x + k) % 4 for k in (2, 1, 3)]

    def zls(self):
        return [(self.zl + k) % 4 for k in (2, 1, 3)]

    def to_features(self):
        return dict(
            zl=3 * self.zh + (self.x % 2) * (1 - 2 * self.zh),
            x=self.y,
            c=1 - self.c,
            zh=self.zl // 2,
            y=(self.zl % 2) * 2 + self.x // 2,
        )

    def to_owner(self):
        return dict(
            zl=self.zh * 2 + self.y // 2,
            x=(self.y % 2) * 2 + ((self.zl + 1) // 2) % 2,
            c=1 - self.c,
            zh=self.zl // 2,
            y=self.x,
        )


class Copies:
    def __init__(self, send_sem, recv_sem):
        self.send_sem, self.recv_sem = send_sem, recv_sem
        self.used = 0
        self.sent = []

    def make(self, source, target, device):
        copy = pltpu.make_async_remote_copy(
            src_ref=source,
            dst_ref=target,
            send_sem=self.send_sem.at[self.used],
            recv_sem=self.recv_sem.at[self.used],
            device_id=device,
            device_id_type=MESH,
        )
        self.used += 1
        return copy

    def send(self, source, target, device):
        copy = self.make(source, target, device)
        copy.start()
        self.sent.append(copy)
        return copy

    def finish(self):
        for copy in self.sent:
            copy.wait_send()


def arrived(copies):
    for copy in copies:
        copy.wait_recv()


def greet(senders, targets):
    barrier = pltpu.get_barrier_semaphore()
    for device in senders:
        pl.semaphore_signal(barrier, inc=1, device_id=device, device_id_type=MESH)
    pl.semaphore_wait(barrier, len(targets))


def part(index, size):
    return pl.ds(pl.multiple_of(index * size, size), size)


def diagonal():
    return lax.broadcasted_iota(jnp.int32, (128, 128), 0) == lax.broadcasted_iota(jnp.int32, (128, 128), 1)


def to_column(row):
    eye = diagonal()
    pieces = [
        jnp.sum(
            jnp.where(eye, jnp.broadcast_to(row[:, k : k + 128], (128, 128)), 0.0), axis=1, keepdims=True
        )
        for k in range(0, row.shape[1], 128)
    ]
    return jnp.concatenate(pieces, axis=0)


def to_row(column):
    eye = diagonal()
    pieces = [
        jnp.sum(
            jnp.where(eye, jnp.broadcast_to(column[k : k + 128], (128, 128)), 0.0), axis=0, keepdims=True
        )
        for k in range(0, column.shape[0], 128)
    ]
    return jnp.concatenate(pieces, axis=1)


def kernel(
    attn_ref, resid_ref, proj_ref, sec_ref, book_ref, dec_ref, head_ref, codes_ref,
    loss_ref, out_ref,
    turned, wd, resid_part, full, pre, mine, sect, decs, book, head, embed, proj_in, logits, dlogits,
    to_scan, got, done, states, carry_in, carry_out,
    gsend, ggot, far_out, far_in, inners, gp, core_got, group, group_got, line, line_got, last,
    send_sem, recv_sem, local_sem, line_send, line_recv,
):
    me = Place()
    copies = Copies(send_sem, recv_sem)
    frames, width = attn_ref.shape
    block = proj_ref.shape[0]
    inner_width = sec_ref.shape[1]
    chunk = inner_width // CHUNKS
    code_count = book.shape[0]
    rows = frames // 4
    half_frames = frames // 2

    local = [
        pltpu.make_async_copy(resid_ref.at[:, part(me.d, width)], resid_part, local_sem.at[0]),
        pltpu.make_async_copy(book_ref, book, local_sem.at[1]),
        pltpu.make_async_copy(head_ref, head, local_sem.at[2]),
    ]
    for copy in local:
        copy.start()
    carry_in[...] = jnp.zeros_like(carry_in)
    decs[me.y] = jnp.broadcast_to(dec_ref[...], decs.shape[1:])
    for j in range(CHUNKS):
        sect[j, me.zl, me.x, me.c] = sec_ref[:, j * chunk : (j + 1) * chunk]
    full[:, part(me.d, width)] = attn_ref[...]

    y_peers = [me.at(y=y) for y in me.ys()]
    x_peers = [me.at(x=x) for x in me.xs()]
    zl_peers = [me.at(zl=zl) for zl in me.zls()]
    right, left = me.at(x=(me.x + 1) % 4), me.at(x=(me.x + 3) % 4)
    far, other = me.at(zh=1 - me.zh), me.at(c=1 - me.c)
    cross = [me.at(zh=1 - me.zh, y=y) for y in me.ys()]
    there, home = me.to_features(), me.to_owner()
    shared = y_peers + x_peers + zl_peers + cross + [far, other]
    both = shared + [me.at(**there), me.at(**home)]
    greet(both, both)

    up, down = me.at(y=(me.y + 1) % 4), me.at(y=(me.y + 3) % 4)

    def piece(buffer, zh, y, k):
        return buffer.at[pl.ds(k * half_frames, half_frames), part(zh * 4 + y, width)]

    def cross_over(buffer, source):
        return [
            copies.send(source.at[pl.ds(k * half_frames, half_frames)], piece(buffer, me.zh, me.y, k), far)
            for k in range(2)
        ]

    def spread(buffer, zh, k, source=None):
        place = piece(buffer, zh, me.y, k)
        source = place if source is None else source.at[pl.ds(k * half_frames, half_frames)]
        return copies.send(source, place, up), copies.send(source, place, down)

    def forward(buffer, zh, k, pair):
        pair[k].wait_recv()
        place = piece(buffer, zh, (me.y + (3, 1)[k]) % 4, k)
        return [copies.send(place, place, (up, down)[k]), pair[1 - k]]

    class Ring:
        def __init__(self, slot, view):
            self.slot, self.view = slot, view
            self.cores = []

        def line(self):
            self.zs = [copies.send(self.slot, self.slot, peer) for peer in zl_peers]

        def first(self):
            arrived(self.zs)
            group = self.view(me.x)
            self.right = copies.send(group, group, right)
            self.left = copies.send(group, group, left)
            self.cores.append(copies.send(group, group, other))

        def second(self):
            self.right.wait_recv()
            x = (me.x + 3) % 4
            self.on_right = copies.send(self.view(x, 0), self.view(x, 0), right)
            self.cores.append(copies.send(self.view(x), self.view(x), other))
            self.left.wait_recv()
            x = (me.x + 1) % 4
            self.on_left = copies.send(self.view(x, 1), self.view(x, 1), left)
            self.cores.append(copies.send(self.view(x), self.view(x), other))

        def third(self):
            arrived([self.on_right, self.on_left])
            group = self.view((me.x + 2) % 4)
            self.cores.append(copies.send(group, group, other))

        def end(self):
            arrived(self.cores)

    half_block = block // 2

    def wd_view(k):
        lines = pl.ds(k * half_block, half_block)

        def view(x, half=None):
            zls = slice(None) if half is None else pl.ds(2 * half, 2)
            return wd.at[zls, x, 1 - me.c, lines]

        return view

    def sect_view(j):
        def view(x, half=None):
            return sect.at[j, :, x, me.c] if half is None else sect.at[j, pl.ds(2 * half, 2), x, me.c]

        return view

    wd_rings = [
        Ring(wd.at[me.zl, me.x, 1 - me.c, pl.ds(k * half_block, half_block)], wd_view(k))
        for k in range(2)
    ]
    sec_rings = [Ring(sect.at[j, me.zl, me.x, me.c], sect_view(j)) for j in range(CHUNKS)]

    moved = copies.send(
        proj_ref, wd.at[there["zl"], there["x"], 1 - there["c"]], me.at(**there)
    )
    sec_rings[0].line()
    moved.wait_recv()
    for ring in wd_rings:
        ring.line()
    attn_near = [spread(full, me.zh, k, attn_ref) for k in range(2)]
    dec_near = [copies.send(decs.at[me.y], decs.at[me.y], peer) for peer in y_peers]
    sec_rings[0].first()
    wd_rings[0].first()
    attn_cross = cross_over(full, attn_ref)
    attn_done = []
    for k in range(2):
        attn_done += forward(full, me.zh, k, attn_near[k])
    sec_rings[0].second()
    wd_rings[1].first()

    codes = codes_ref[...].astype(F32)
    code_rows = lax.broadcasted_iota(jnp.int32, codes.shape, 0)
    lanes = lax.broadcasted_iota(jnp.int32, (1, frames), 1)
    target = to_column(jnp.sum(jnp.where(code_rows == me.d, codes, 0.0), axis=0, keepdims=True))
    before = jnp.sum(jnp.where(code_rows == me.d - 1, codes, 0.0), axis=0, keepdims=True)
    shifted = pltpu.roll(codes, 1, 1)[codes.shape[0] - 1 :]
    shifted = jnp.where(lanes % LENGTH == 0, -1.0, shifted)
    previous = to_column(jnp.where(me.d == 0, shifted, before))
    code_lanes = lax.broadcasted_iota(jnp.int32, (frames, code_count), 1).astype(F32)
    for copy in local:
        copy.wait()
    embed[...] = jnp.dot(
        jnp.where(code_lanes == previous, 1.0, 0.0).astype(BF), book[...], preferred_element_type=F32
    )

    sec_rings[1].line()
    wd_rings[0].second()
    attn_far = []
    for k in range(2):
        attn_cross[k].wait_recv()
        attn_far.append(spread(full, 1 - me.zh, k))
    wd_rings[1].second()
    sec_rings[2].line()
    sec_rings[3].line()
    sec_rings[0].third()
    attn_done += forward(full, 1 - me.zh, 0, attn_far[0])
    wd_rings[0].third()
    attn_done += forward(full, 1 - me.zh, 1, attn_far[1])
    wd_rings[1].third()
    sec_rings[1].first()
    for ring in wd_rings:
        ring.end()
    arrived(attn_done)

    for u in range(2):
        total = jnp.zeros((frames, 2 * block), F32)
        for h in range(8):
            weight = wd[PAIRS[u][h // 4], h % 4].reshape(2 * block, width)
            total += lax.dot_general(
                full[:, h * width : (h + 1) * width], weight, NT, preferred_element_type=F32
            )
        features = pl.ds(u * 2 * block, 2 * block)
        mine[:, features] = (resid_part[:, features].astype(F32) + total).astype(BF)
    pre[:, part(me.d, width)] = mine[...]
    pre_cross = cross_over(pre, mine)
    pre_near = [spread(pre, me.zh, k, mine) for k in range(2)]

    def squares(zh):
        value = pre[:, part(zh, 4 * width)].astype(F32)
        return jnp.sum(value * value, axis=1, keepdims=True)

    def projection(j, zh):
        weight = sect[j, pl.ds(2 * zh, 2)].reshape(4 * width, chunk)
        return jnp.dot(pre[:, part(zh, 4 * width)], weight, preferred_element_type=F32)

    sec_rings[1].second()
    sec_rings[2].first()
    sec_rings[3].first()
    pre_near_done, pre_far, pre_far_done = [], [], []
    for k in range(2):
        pre_near_done += forward(pre, me.zh, k, pre_near[k])
    pre_cross[0].wait_recv()
    pre_far.append(spread(pre, 1 - me.zh, 0))
    sec_rings[1].third()
    sec_rings[2].second()
    pre_cross[1].wait_recv()
    pre_far.append(spread(pre, 1 - me.zh, 1))
    sec_rings[2].third()
    sec_rings[3].second()
    for k in range(2):
        pre_far_done += forward(pre, 1 - me.zh, k, pre_far[k])
    arrived(pre_near_done)
    mean = squares(me.zh)
    for j in range(3):
        sec_rings[j].end()
        proj_in[j] = projection(j, me.zh)
    arrived(pre_far_done + dec_near)
    mean += squares(1 - me.zh)
    factor = lax.rsqrt(mean * (1.0 / pre.shape[1]) + EPSILON)

    def exchange(backward, value):
        way = 1 if backward else 0
        first = 1 if backward else 0
        sent = []
        for j in range(CHUNKS):
            to_scan[way, j] = value(j).astype(BF)
            sent.append(
                [copies.send(to_scan.at[way, j, part(y, rows)], got.at[way, j, me.y], me.at(y=y)) for y in me.ys()]
            )
            got[way, j, me.y] = to_scan[way, j, part(me.y, rows)]
        returned, carries = [], []
        for j in range(CHUNKS):
            arrived(sent[j])
            carry = copies.make(carry_out.at[way, j], carry_in.at[way, j], far)
            carries.append(carry)

            @pl.when(me.zh != first)
            def _(carry=carry):
                carry.wait_recv()

            state = carry_in[way, j].astype(F32)
            for section in reversed(range(4)) if backward else range(4):
                decay = decs[section, 0:1, j * chunk : (j + 1) * chunk]
                if backward:
                    here = got[way, j, section].astype(F32) + state
                    done[way, j, section] = here.astype(BF)
                    state = decay * here
                else:
                    state = decay * state + got[way, j, section].astype(F32)
                    done[way, j, section] = state.astype(BF)
            carry_out[way, j] = state.astype(BF)

            @pl.when(me.zh == first)
            def _(carry=carry):
                carry.start()

            returned.append(
                [copies.send(done.at[way, j, y], states.at[way, j, part(me.y, rows)], me.at(y=y)) for y in me.ys()]
            )
            states[way, j, part(me.y, rows)] = done[way, j, me.y]
        return returned, carries, first

    def entering(j):
        if j == 3:
            sec_rings[3].third()
            sec_rings[3].end()
            proj_in[j] = projection(j, me.zh)
        value = proj_in[j] + projection(j, 1 - me.zh)
        proj_in[j] = value
        return value * factor + embed[:, j * chunk : (j + 1) * chunk]

    returned, carries, first = exchange(False, entering)

    mean = jnp.zeros((frames, 1), F32)
    for j in range(CHUNKS):
        arrived(returned[j])
        value = states[0, j]
        wide = value.astype(F32)
        mean += jnp.sum(wide * wide, axis=1, keepdims=True)
        term = jnp.dot(value, head[j * chunk : (j + 1) * chunk], preferred_element_type=F32)
        logits[...] = term if j == 0 else logits[...] + term
    norm = lax.rsqrt(mean * (1.0 / inner_width) + EPSILON)
    loss_parts, inner_parts = [], []
    step = 64
    for start in range(0, frames, step):
        piece = pl.ds(start, step)
        value = logits[piece] * norm[start : start + step]
        chosen = lax.broadcasted_iota(jnp.int32, (step, code_count), 1).astype(F32) == target[start : start + step]
        top = jnp.max(value, axis=1, keepdims=True)
        raised = jnp.exp(value - top)
        total = jnp.sum(raised, axis=1, keepdims=True)
        picked = jnp.sum(jnp.where(chosen, value, 0.0), axis=1, keepdims=True)
        loss_parts.append(top + jnp.log(total) - picked)
        slope = (raised * (1.0 / total) - jnp.where(chosen, 1.0, 0.0)).astype(BF)
        dlogits[piece] = slope
        inner_parts.append(jnp.sum(slope.astype(F32) * value, axis=1, keepdims=True))
    loss_ref[...] = to_row(jnp.concatenate(loss_parts, axis=0))
    inner = jnp.concatenate(inner_parts, axis=0) * (1.0 / inner_width)

    def leaving(j):
        value = lax.dot_general(
            dlogits[...], head[j * chunk : (j + 1) * chunk], NT, preferred_element_type=F32
        )
        return norm * (value - states[0, j].astype(F32) * (norm * inner))

    returned, more, last_first = exchange(True, leaving)

    inner = jnp.zeros((frames, 1), F32)
    for j in range(CHUNKS):
        arrived(returned[j])
        inner += jnp.sum(states[1, j].astype(F32) * proj_in[j], axis=1, keepdims=True)
    inners[me.d] = jnp.broadcast_to(to_row(inner), inners.shape[1:])
    inner_sent = [copies.send(inners.at[me.d], inners.at[me.d], peer) for peer in y_peers + [far] + cross]

    def term(u, zh, y):
        d = zh * 4 + y
        total = jnp.zeros((frames, 2 * block), F32)
        for j in range(CHUNKS):
            weight = sect[j, d // 2, (d % 2) * 2 + u].reshape(2 * block, chunk)
            total += lax.dot_general(states[1, j], weight, NT, preferred_element_type=F32)
        return total

    sums, kept = {}, {}
    order = me.xs() + [me.x]
    for u in range(2):
        for k, zh in enumerate((1 - me.zh, me.zh)):
            for slot, y in enumerate(me.ys()):
                value = term(u, zh, y).astype(BF)
                for lo in range(2):
                    gsend[2 * u + lo, k, slot] = value[:, lo * block : (lo + 1) * block]
            kept[u, k] = term(u, zh, me.y)
            sums[2 * u, k] = [
                copies.send(gsend.at[2 * u, k, slot], ggot.at[2 * u, k, slot], me.at(y=y))
                for slot, y in enumerate(me.ys())
            ]
        for k in range(2):
            sums[2 * u + 1, k] = [
                copies.send(gsend.at[2 * u + 1, k, slot], ggot.at[2 * u + 1, k, slot], me.at(y=y))
                for slot, y in enumerate(me.ys())
            ]

    along = [
        [
            [copies.make(group.at[hi, x, zh], group_got.at[slot, hi, zh], me.at(x=x)) for zh in range(2)]
            for slot, x in enumerate(order[:3])
        ]
        for hi in range(2)
    ]
    in_core = [[copies.make(gp.at[q, x], core_got.at[q // 2, x], other) for x in order] for q in range(4)]

    def reduced(q, k):
        lo = q % 2
        total = kept[q // 2, k][:, lo * block : (lo + 1) * block]
        for slot, copy in enumerate(sums[q, k]):
            copy.wait_recv()
            total += ggot[q, k, slot].astype(F32)
        return total

    def cross_part(q):
        far_out[q] = reduced(q, 0).astype(BF)
        return copies.send(far_out.at[q], far_in.at[q], far)

    crossing = [cross_part(0)]
    for q in range(4):
        total = reduced(q, 1)
        if q < 3:
            crossing.append(cross_part(q + 1))
        if q == 0:
            arrived(inner_sent)
            inner = to_column(jnp.sum(inners[...], axis=0)[0:1])
            scale = factor * factor * factor * inner * (1.0 / pre.shape[1])
        crossing[q].wait_recv()
        total += far_in[q].astype(F32)
        dpre = factor * total - mine[:, q * block : (q + 1) * block].astype(F32) * scale
        turned[q] = dpre.T.astype(BF)

        for slot, x in enumerate(order):
            for zh in range(2):
                gp[q, x, zh] = jnp.dot(
                    turned[q], full[:, part(zh * 4 + x, width)], preferred_element_type=F32
                ).astype(BF)

            @pl.when(me.c == q % 2)
            def _(copy=in_core[q][slot]):
                copy.start()

        @pl.when(me.c != q % 2)
        def _(q=q, hi=q // 2):
            for slot, x in enumerate(order):
                in_core[q][slot].wait_recv()
                for zh in range(2):
                    group[hi, x, zh] = (gp[q, x, zh].astype(F32) + core_got[hi, x, zh].astype(F32)).astype(BF)
                    if slot < 3:
                        along[hi][slot][zh].start()

    def line_copy(zl):
        return pltpu.make_async_remote_copy(
            src_ref=line.at[zl],
            dst_ref=line_got.at[me.zl],
            send_sem=line_send.at[zl],
            recv_sem=line_recv.at[me.zl],
            device_id=me.at(zl=zl),
            device_id_type=MESH,
        )

    for hi, zh in ((0, 0), (0, 1), (1, 0), (1, 1)):
        zl = PAIRS[hi][zh]
        value = group[hi, me.x, zh].astype(F32)
        for slot in range(3):
            along[hi][slot][zh].wait_recv()
            value += group_got[slot, hi, zh].astype(F32)
        line[zl] = value.astype(BF)

        @pl.when(me.zl != zl)
        def _(zl=zl):
            line_copy(zl).start()

    value = line[me.zl].astype(F32)
    for k in range(1, 4):
        zl = (me.zl + k) % 4
        pltpu.make_async_remote_copy(
            src_ref=line.at[zl],
            dst_ref=line_got.at[zl],
            send_sem=line_send.at[zl],
            recv_sem=line_recv.at[zl],
            device_id=me.at(zl=zl),
            device_id_type=MESH,
        ).wait_recv()
        value += line_got[zl].astype(F32)
    last[...] = value.astype(BF)
    ending = copies.send(last, out_ref, me.at(**home))
    for zl in range(4):

        @pl.when(me.zl != zl)
        def _(zl=zl):
            line_copy(zl).wait_send()

    for q in range(4):

        @pl.when(me.c == q % 2)
        def _(q=q):
            for copy in in_core[q]:
                copy.wait_send()

    for side in along:
        for slot in side:
            for copy in slot:
                copy.wait_send()
    for made, start_at in ((carries, first), (more, last_first)):

        @pl.when(me.zh == start_at)
        def _(made=made):
            for copy in made:
                copy.wait_send()

    copies.finish()
    ending.wait_recv()


def local(attn_out, resid, out_proj, section_in, codebook, decays, section_out, codes):
    frames, width = attn_out.shape
    block = out_proj.shape[0]
    _, rows_in, inner = section_in.shape
    code_count = codebook.shape[1]
    chunk = inner // CHUNKS
    rows = frames // 4
    vmem = pl.BlockSpec(memory_space=pltpu.VMEM)
    anywhere = pl.BlockSpec(memory_space=pl.ANY)
    copies = 256
    return pl.pallas_call(
        kernel,
        out_shape=(
            jax.ShapeDtypeStruct((1, frames), F32),
            jax.ShapeDtypeStruct((block, width), BF),
        ),
        in_specs=[vmem, anywhere, vmem, vmem, anywhere, vmem, anywhere, vmem],
        out_specs=[vmem, vmem],
        scratch_shapes=[
            pltpu.VMEM((4, block, frames), BF),
            pltpu.VMEM((4, 4, 2, block, width), BF),
            pltpu.VMEM((frames, width), BF),
            pltpu.VMEM((frames, 8 * width), BF),
            pltpu.VMEM((frames, 8 * width), BF),
            pltpu.VMEM((frames, width), BF),
            pltpu.VMEM((CHUNKS, 4, 4, 2, rows_in, chunk), BF),
            pltpu.VMEM((4, 8, inner), F32),
            pltpu.VMEM((code_count, inner), BF),
            pltpu.VMEM((inner, code_count), BF),
            pltpu.VMEM((frames, inner), F32),
            pltpu.VMEM((CHUNKS, frames, chunk), F32),
            pltpu.VMEM((frames, code_count), F32),
            pltpu.VMEM((frames, code_count), BF),
            pltpu.VMEM((2, CHUNKS, frames, chunk), BF),
            pltpu.VMEM((2, CHUNKS, 4, rows, chunk), BF),
            pltpu.VMEM((2, CHUNKS, 4, rows, chunk), BF),
            pltpu.VMEM((2, CHUNKS, frames, chunk), BF),
            pltpu.VMEM((2, CHUNKS, rows, chunk), BF),
            pltpu.VMEM((2, CHUNKS, rows, chunk), BF),
            pltpu.VMEM((4, 2, 3, frames, block), BF),
            pltpu.VMEM((4, 2, 3, frames, block), BF),
            pltpu.VMEM((4, frames, block), BF),
            pltpu.VMEM((4, frames, block), BF),
            pltpu.VMEM((8, 8, frames), F32),
            pltpu.VMEM((4, 4, 2, block, width), BF),
            pltpu.VMEM((2, 4, 2, block, width), BF),
            pltpu.VMEM((2, 4, 2, block, width), BF),
            pltpu.VMEM((3, 2, 2, block, width), BF),
            pltpu.VMEM((4, block, width), BF),
            pltpu.VMEM((4, block, width), BF),
            pltpu.VMEM((block, width), BF),
            pltpu.SemaphoreType.DMA((copies,)),
            pltpu.SemaphoreType.DMA((copies,)),
            pltpu.SemaphoreType.DMA((3,)),
            pltpu.SemaphoreType.DMA((4,)),
            pltpu.SemaphoreType.DMA((4,)),
        ],
        compiler_params=pltpu.CompilerParams(
            collective_id=0, has_side_effects=True, vmem_limit_bytes=VMEM_LIMIT
        ),
        name="whole",
    )(attn_out, resid, out_proj, section_in[0], codebook[0], decays, section_out[0], codes)


def solution(mesh):
    return jax.shard_map(
        local,
        mesh=mesh,
        in_specs=(
            P("wide", "depth"),
            P("wide", None),
            P("wide", "depth"),
            P("depth", "wide", None),
            P("depth", None, None),
            P("depth", None),
            P("depth", None, None),
            P(None, "wide"),
        ),
        out_specs=(P("depth", "wide"), P("wide", "depth")),
        check_vma=False,
    )
```

```python
import jax
import jax.numpy as jnp
from jax import lax
from jax.experimental import pallas as pl
from jax.experimental.pallas import tpu as pltpu
from jax.sharding import PartitionSpec as P

MESH = pl.DeviceIdType.MESH
LENGTH = 256
EPSILON = 1e-06
BF = jnp.bfloat16
F32 = jnp.float32
VMEM_LIMIT = 56 << 20
CHUNKS = 4
PAIRS = ((0, 3), (1, 2))
NT = (((1,), (1,)), ((), ()))


class Place:
    def __init__(self):
        w, d = lax.axis_index("wide"), lax.axis_index("depth")
        self.zl, self.x, self.c = w // 8, (w // 2) % 4, w % 2
        self.zh, self.y = d // 4, d % 4
        self.d = d

    def at(self, zl=None, x=None, c=None, zh=None, y=None):
        zl = self.zl if zl is None else zl
        x = self.x if x is None else x
        c = self.c if c is None else c
        zh = self.zh if zh is None else zh
        y = self.y if y is None else y
        return (zl * 8 + x * 2 + c, zh * 4 + y)

    def ys(self):
        return [(self.y + k) % 4 for k in (2, 1, 3)]

    def xs(self):
        return [(self.x + k) % 4 for k in (2, 1, 3)]

    def zls(self):
        return [(self.zl + k) % 4 for k in (2, 1, 3)]

    def to_features(self):
        return dict(
            zl=3 * self.zh + (self.x % 2) * (1 - 2 * self.zh),
            x=self.y,
            c=1 - self.c,
            zh=self.zl // 2,
            y=(self.zl % 2) * 2 + self.x // 2,
        )

    def to_owner(self):
        return dict(
            zl=self.zh * 2 + self.y // 2,
            x=(self.y % 2) * 2 + ((self.zl + 1) // 2) % 2,
            c=1 - self.c,
            zh=self.zl // 2,
            y=self.x,
        )


class Copies:
    def __init__(self, send_sem, recv_sem):
        self.send_sem, self.recv_sem = send_sem, recv_sem
        self.used = 0
        self.sent = []

    def make(self, source, target, device):
        copy = pltpu.make_async_remote_copy(
            src_ref=source,
            dst_ref=target,
            send_sem=self.send_sem.at[self.used],
            recv_sem=self.recv_sem.at[self.used],
            device_id=device,
            device_id_type=MESH,
        )
        self.used += 1
        return copy

    def send(self, source, target, device):
        copy = self.make(source, target, device)
        copy.start()
        self.sent.append(copy)
        return copy

    def finish(self):
        for copy in self.sent:
            copy.wait_send()


def arrived(copies):
    for copy in copies:
        copy.wait_recv()


def greet(senders, targets):
    barrier = pltpu.get_barrier_semaphore()
    for device in senders:
        pl.semaphore_signal(barrier, inc=1, device_id=device, device_id_type=MESH)
    pl.semaphore_wait(barrier, len(targets))


def part(index, size):
    return pl.ds(pl.multiple_of(index * size, size), size)


def diagonal():
    return lax.broadcasted_iota(jnp.int32, (128, 128), 0) == lax.broadcasted_iota(jnp.int32, (128, 128), 1)


def to_column(row):
    eye = diagonal()
    pieces = [
        jnp.sum(
            jnp.where(eye, jnp.broadcast_to(row[:, k : k + 128], (128, 128)), 0.0), axis=1, keepdims=True
        )
        for k in range(0, row.shape[1], 128)
    ]
    return jnp.concatenate(pieces, axis=0)


def to_row(column):
    eye = diagonal()
    pieces = [
        jnp.sum(
            jnp.where(eye, jnp.broadcast_to(column[k : k + 128], (128, 128)), 0.0), axis=0, keepdims=True
        )
        for k in range(0, column.shape[0], 128)
    ]
    return jnp.concatenate(pieces, axis=1)


def kernel(
    attn_ref, resid_ref, proj_ref, sec_ref, book_ref, dec_ref, head_ref, codes_ref,
    loss_ref, out_ref,
    turned, wd, resid_part, full, pre, mine, sect, decs, book, head, embed, proj_in, logits, dlogits,
    to_scan, got, done, states, carry_in, carry_out,
    gsend, ggot, far_out, far_in, inners, gp, core_got, group, group_got, line, line_got, last,
    send_sem, recv_sem, local_sem, line_send, line_recv,
):
    me = Place()
    copies = Copies(send_sem, recv_sem)
    frames, width = attn_ref.shape
    block = proj_ref.shape[0]
    inner_width = sec_ref.shape[1]
    chunk = inner_width // CHUNKS
    code_count = book.shape[0]
    rows = frames // 4
    half_frames = frames // 2

    local = [
        pltpu.make_async_copy(resid_ref.at[:, part(me.d, width)], resid_part, local_sem.at[0]),
        pltpu.make_async_copy(book_ref, book, local_sem.at[1]),
        pltpu.make_async_copy(head_ref, head, local_sem.at[2]),
    ]
    for copy in local:
        copy.start()
    carry_in[...] = jnp.zeros_like(carry_in)
    decs[me.y] = jnp.broadcast_to(dec_ref[...], decs.shape[1:])
    for j in range(CHUNKS):
        sect[j, me.zl, me.x, me.c] = sec_ref[:, j * chunk : (j + 1) * chunk]
    full[:, part(me.d, width)] = attn_ref[...]

    y_peers = [me.at(y=y) for y in me.ys()]
    x_peers = [me.at(x=x) for x in me.xs()]
    zl_peers = [me.at(zl=zl) for zl in me.zls()]
    right, left = me.at(x=(me.x + 1) % 4), me.at(x=(me.x + 3) % 4)
    far, other = me.at(zh=1 - me.zh), me.at(c=1 - me.c)
    cross = [me.at(zh=1 - me.zh, y=y) for y in me.ys()]
    there, home = me.to_features(), me.to_owner()
    shared = y_peers + x_peers + zl_peers + cross + [far, other]
    both = shared + [me.at(**there), me.at(**home)]
    greet(both, both)

    up, down = me.at(y=(me.y + 1) % 4), me.at(y=(me.y + 3) % 4)

    def piece(buffer, zh, y, k):
        return buffer.at[pl.ds(k * half_frames, half_frames), part(zh * 4 + y, width)]

    def cross_over(buffer, source):
        return [
            copies.send(source.at[pl.ds(k * half_frames, half_frames)], piece(buffer, me.zh, me.y, k), far)
            for k in range(2)
        ]

    def spread(buffer, zh, k, source=None):
        place = piece(buffer, zh, me.y, k)
        source = place if source is None else source.at[pl.ds(k * half_frames, half_frames)]
        return copies.send(source, place, up), copies.send(source, place, down)

    def forward(buffer, zh, k, pair):
        pair[k].wait_recv()
        place = piece(buffer, zh, (me.y + (3, 1)[k]) % 4, k)
        return [copies.send(place, place, (up, down)[k]), pair[1 - k]]

    class Ring:
        def __init__(self, slot, view):
            self.slot, self.view = slot, view
            self.cores = []

        def line(self):
            self.zs = [copies.send(self.slot, self.slot, peer) for peer in zl_peers]

        def first(self):
            arrived(self.zs)
            group = self.view(me.x)
            self.right = copies.send(group, group, right)
            self.left = copies.send(group, group, left)
            self.cores.append(copies.send(group, group, other))

        def second(self):
            self.right.wait_recv()
            x = (me.x + 3) % 4
            self.on_right = copies.send(self.view(x, 0), self.view(x, 0), right)
            self.cores.append(copies.send(self.view(x), self.view(x), other))
            self.left.wait_recv()
            x = (me.x + 1) % 4
            self.on_left = copies.send(self.view(x, 1), self.view(x, 1), left)
            self.cores.append(copies.send(self.view(x), self.view(x), other))

        def third(self):
            arrived([self.on_right, self.on_left])
            group = self.view((me.x + 2) % 4)
            self.cores.append(copies.send(group, group, other))

        def end(self):
            arrived(self.cores)

    half_block = block // 2

    def wd_view(k):
        lines = pl.ds(k * half_block, half_block)

        def view(x, half=None):
            zls = slice(None) if half is None else pl.ds(2 * half, 2)
            return wd.at[zls, x, 1 - me.c, lines]

        return view

    def sect_view(j):
        def view(x, half=None):
            return sect.at[j, :, x, me.c] if half is None else sect.at[j, pl.ds(2 * half, 2), x, me.c]

        return view

    wd_rings = [
        Ring(wd.at[me.zl, me.x, 1 - me.c, pl.ds(k * half_block, half_block)], wd_view(k))
        for k in range(2)
    ]
    sec_rings = [Ring(sect.at[j, me.zl, me.x, me.c], sect_view(j)) for j in range(CHUNKS)]

    moved = copies.send(
        proj_ref, wd.at[there["zl"], there["x"], 1 - there["c"]], me.at(**there)
    )
    sec_rings[0].line()
    moved.wait_recv()
    for ring in wd_rings:
        ring.line()
    attn_near = [spread(full, me.zh, k, attn_ref) for k in range(2)]
    dec_near = [copies.send(decs.at[me.y], decs.at[me.y], peer) for peer in y_peers]
    sec_rings[0].first()
    wd_rings[0].first()
    attn_cross = cross_over(full, attn_ref)
    attn_done = []
    for k in range(2):
        attn_done += forward(full, me.zh, k, attn_near[k])
    sec_rings[0].second()
    wd_rings[1].first()

    codes = codes_ref[...].astype(F32)
    code_rows = lax.broadcasted_iota(jnp.int32, codes.shape, 0)
    lanes = lax.broadcasted_iota(jnp.int32, (1, frames), 1)
    target = to_column(jnp.sum(jnp.where(code_rows == me.d, codes, 0.0), axis=0, keepdims=True))
    before = jnp.sum(jnp.where(code_rows == me.d - 1, codes, 0.0), axis=0, keepdims=True)
    shifted = pltpu.roll(codes, 1, 1)[codes.shape[0] - 1 :]
    shifted = jnp.where(lanes % LENGTH == 0, -1.0, shifted)
    previous = to_column(jnp.where(me.d == 0, shifted, before))
    code_lanes = lax.broadcasted_iota(jnp.int32, (frames, code_count), 1).astype(F32)
    for copy in local:
        copy.wait()
    embed[...] = jnp.dot(
        jnp.where(code_lanes == previous, 1.0, 0.0).astype(BF), book[...], preferred_element_type=F32
    )

    sec_rings[1].line()
    wd_rings[0].second()
    attn_far = []
    for k in range(2):
        attn_cross[k].wait_recv()
        attn_far.append(spread(full, 1 - me.zh, k))
    wd_rings[1].second()
    sec_rings[2].line()
    sec_rings[3].line()
    sec_rings[0].third()
    attn_done += forward(full, 1 - me.zh, 0, attn_far[0])
    wd_rings[0].third()
    attn_done += forward(full, 1 - me.zh, 1, attn_far[1])
    wd_rings[1].third()
    sec_rings[1].first()
    for ring in wd_rings:
        ring.end()
    arrived(attn_done)

    for u in range(2):
        total = jnp.zeros((frames, 2 * block), F32)
        for h in range(8):
            weight = wd[PAIRS[u][h // 4], h % 4].reshape(2 * block, width)
            total += lax.dot_general(
                full[:, h * width : (h + 1) * width], weight, NT, preferred_element_type=F32
            )
        features = pl.ds(u * 2 * block, 2 * block)
        mine[:, features] = (resid_part[:, features].astype(F32) + total).astype(BF)
    pre[:, part(me.d, width)] = mine[...]
    pre_cross = cross_over(pre, mine)
    pre_near = [spread(pre, me.zh, k, mine) for k in range(2)]

    def squares(zh):
        value = pre[:, part(zh, 4 * width)].astype(F32)
        return jnp.sum(value * value, axis=1, keepdims=True)

    def projection(j, zh):
        weight = sect[j, pl.ds(2 * zh, 2)].reshape(4 * width, chunk)
        return jnp.dot(pre[:, part(zh, 4 * width)], weight, preferred_element_type=F32)

    sec_rings[1].second()
    sec_rings[2].first()
    sec_rings[3].first()
    pre_near_done, pre_far, pre_far_done = [], [], []
    for k in range(2):
        pre_near_done += forward(pre, me.zh, k, pre_near[k])
    pre_cross[0].wait_recv()
    pre_far.append(spread(pre, 1 - me.zh, 0))
    sec_rings[1].third()
    sec_rings[2].second()
    pre_cross[1].wait_recv()
    pre_far.append(spread(pre, 1 - me.zh, 1))
    sec_rings[2].third()
    sec_rings[3].second()
    for k in range(2):
        pre_far_done += forward(pre, 1 - me.zh, k, pre_far[k])
    arrived(pre_near_done)
    mean = squares(me.zh)
    for j in range(3):
        sec_rings[j].end()
        proj_in[j] = projection(j, me.zh)
    arrived(pre_far_done + dec_near)
    mean += squares(1 - me.zh)
    factor = lax.rsqrt(mean * (1.0 / pre.shape[1]) + EPSILON)

    def exchange(backward, value):
        way = 1 if backward else 0
        first = 1 if backward else 0
        sent = []
        for j in range(CHUNKS):
            to_scan[way, j] = value(j).astype(BF)
            sent.append(
                [copies.send(to_scan.at[way, j, part(y, rows)], got.at[way, j, me.y], me.at(y=y)) for y in me.ys()]
            )
            got[way, j, me.y] = to_scan[way, j, part(me.y, rows)]
        returned, carries = [], []
        for j in range(CHUNKS):
            arrived(sent[j])
            carry = copies.make(carry_out.at[way, j], carry_in.at[way, j], far)
            carries.append(carry)

            @pl.when(me.zh != first)
            def _(carry=carry):
                carry.wait_recv()

            state = carry_in[way, j].astype(F32)
            for section in reversed(range(4)) if backward else range(4):
                decay = decs[section, 0:1, j * chunk : (j + 1) * chunk]
                if backward:
                    here = got[way, j, section].astype(F32) + state
                    done[way, j, section] = here.astype(BF)
                    state = decay * here
                else:
                    state = decay * state + got[way, j, section].astype(F32)
                    done[way, j, section] = state.astype(BF)
            carry_out[way, j] = state.astype(BF)

            @pl.when(me.zh == first)
            def _(carry=carry):
                carry.start()

            returned.append(
                [copies.send(done.at[way, j, y], states.at[way, j, part(me.y, rows)], me.at(y=y)) for y in me.ys()]
            )
            states[way, j, part(me.y, rows)] = done[way, j, me.y]
        return returned, carries, first

    def entering(j):
        if j == 3:
            sec_rings[3].third()
            sec_rings[3].end()
            proj_in[j] = projection(j, me.zh)
        value = proj_in[j] + projection(j, 1 - me.zh)
        proj_in[j] = value
        return value * factor + embed[:, j * chunk : (j + 1) * chunk]

    returned, carries, first = exchange(False, entering)

    mean = jnp.zeros((frames, 1), F32)
    for j in range(CHUNKS):
        arrived(returned[j])
        value = states[0, j]
        wide = value.astype(F32)
        mean += jnp.sum(wide * wide, axis=1, keepdims=True)
        term = jnp.dot(value, head[j * chunk : (j + 1) * chunk], preferred_element_type=F32)
        logits[...] = term if j == 0 else logits[...] + term
    norm = lax.rsqrt(mean * (1.0 / inner_width) + EPSILON)
    loss_parts, inner_parts = [], []
    step = 128
    for start in range(0, frames, step):
        piece = pl.ds(start, step)
        value = logits[piece] * norm[start : start + step]
        chosen = lax.broadcasted_iota(jnp.int32, (step, code_count), 1).astype(F32) == target[start : start + step]
        top = jnp.max(value, axis=1, keepdims=True)
        raised = jnp.exp(value - top)
        total = jnp.sum(raised, axis=1, keepdims=True)
        picked = jnp.sum(jnp.where(chosen, value, 0.0), axis=1, keepdims=True)
        loss_parts.append(top + jnp.log(total) - picked)
        slope = (raised * (1.0 / total) - jnp.where(chosen, 1.0, 0.0)).astype(BF)
        dlogits[piece] = slope
        inner_parts.append(jnp.sum(slope.astype(F32) * value, axis=1, keepdims=True))
    loss_ref[...] = to_row(jnp.concatenate(loss_parts, axis=0))
    inner = jnp.concatenate(inner_parts, axis=0) * (1.0 / inner_width)

    def leaving(j):
        value = lax.dot_general(
            dlogits[...], head[j * chunk : (j + 1) * chunk], NT, preferred_element_type=F32
        )
        return norm * (value - states[0, j].astype(F32) * (norm * inner))

    returned, more, last_first = exchange(True, leaving)

    inner = jnp.zeros((frames, 1), F32)
    for j in range(CHUNKS):
        arrived(returned[j])
        inner += jnp.sum(states[1, j].astype(F32) * proj_in[j], axis=1, keepdims=True)
    inners[me.d] = jnp.broadcast_to(to_row(inner), inners.shape[1:])
    inner_sent = [copies.send(inners.at[me.d], inners.at[me.d], peer) for peer in y_peers + [far] + cross]

    def term(u, zh, y):
        d = zh * 4 + y
        total = jnp.zeros((frames, 2 * block), F32)
        for j in range(CHUNKS):
            weight = sect[j, d // 2, (d % 2) * 2 + u].reshape(2 * block, chunk)
            total += lax.dot_general(states[1, j], weight, NT, preferred_element_type=F32)
        return total

    sums, kept = {}, {}
    order = me.xs() + [me.x]
    for u in range(2):
        for k, zh in enumerate((1 - me.zh, me.zh)):
            for slot, y in enumerate(me.ys()):
                value = term(u, zh, y).astype(BF)
                for lo in range(2):
                    gsend[2 * u + lo, k, slot] = value[:, lo * block : (lo + 1) * block]
            kept[u, k] = term(u, zh, me.y)
            sums[2 * u, k] = [
                copies.send(gsend.at[2 * u, k, slot], ggot.at[2 * u, k, slot], me.at(y=y))
                for slot, y in enumerate(me.ys())
            ]
        for k in range(2):
            sums[2 * u + 1, k] = [
                copies.send(gsend.at[2 * u + 1, k, slot], ggot.at[2 * u + 1, k, slot], me.at(y=y))
                for slot, y in enumerate(me.ys())
            ]

    along = [
        [
            [copies.make(group.at[hi, x, zh], group_got.at[slot, hi, zh], me.at(x=x)) for zh in range(2)]
            for slot, x in enumerate(order[:3])
        ]
        for hi in range(2)
    ]
    in_core = [[copies.make(gp.at[q, x], core_got.at[q // 2, x], other) for x in order] for q in range(4)]

    def reduced(q, k):
        lo = q % 2
        total = kept[q // 2, k][:, lo * block : (lo + 1) * block]
        for slot, copy in enumerate(sums[q, k]):
            copy.wait_recv()
            total += ggot[q, k, slot].astype(F32)
        return total

    def cross_part(q):
        far_out[q] = reduced(q, 0).astype(BF)
        return copies.send(far_out.at[q], far_in.at[q], far)

    crossing = [cross_part(0)]
    for q in range(4):
        total = reduced(q, 1)
        if q < 3:
            crossing.append(cross_part(q + 1))
        if q == 0:
            arrived(inner_sent)
            inner = to_column(jnp.sum(inners[...], axis=0)[0:1])
            scale = factor * factor * factor * inner * (1.0 / pre.shape[1])
        crossing[q].wait_recv()
        total += far_in[q].astype(F32)
        dpre = factor * total - mine[:, q * block : (q + 1) * block].astype(F32) * scale
        turned[q] = dpre.T.astype(BF)

        for slot, x in enumerate(order):
            for zh in range(2):
                gp[q, x, zh] = jnp.dot(
                    turned[q], full[:, part(zh * 4 + x, width)], preferred_element_type=F32
                ).astype(BF)

            @pl.when(me.c == q % 2)
            def _(copy=in_core[q][slot]):
                copy.start()

        @pl.when(me.c != q % 2)
        def _(q=q, hi=q // 2):
            for slot, x in enumerate(order):
                in_core[q][slot].wait_recv()
                for zh in range(2):
                    group[hi, x, zh] = (gp[q, x, zh].astype(F32) + core_got[hi, x, zh].astype(F32)).astype(BF)
                    if slot < 3:
                        along[hi][slot][zh].start()

    def line_copy(zl):
        return pltpu.make_async_remote_copy(
            src_ref=line.at[zl],
            dst_ref=line_got.at[me.zl],
            send_sem=line_send.at[zl],
            recv_sem=line_recv.at[me.zl],
            device_id=me.at(zl=zl),
            device_id_type=MESH,
        )

    for hi, zh in ((0, 0), (0, 1), (1, 0), (1, 1)):
        zl = PAIRS[hi][zh]
        value = group[hi, me.x, zh].astype(F32)
        for slot in range(3):
            along[hi][slot][zh].wait_recv()
            value += group_got[slot, hi, zh].astype(F32)
        line[zl] = value.astype(BF)

        @pl.when(me.zl != zl)
        def _(zl=zl):
            line_copy(zl).start()

    value = line[me.zl].astype(F32)
    for k in range(1, 4):
        zl = (me.zl + k) % 4
        pltpu.make_async_remote_copy(
            src_ref=line.at[zl],
            dst_ref=line_got.at[zl],
            send_sem=line_send.at[zl],
            recv_sem=line_recv.at[zl],
            device_id=me.at(zl=zl),
            device_id_type=MESH,
        ).wait_recv()
        value += line_got[zl].astype(F32)
    last[...] = value.astype(BF)
    ending = copies.send(last, out_ref, me.at(**home))
    for zl in range(4):

        @pl.when(me.zl != zl)
        def _(zl=zl):
            line_copy(zl).wait_send()

    for q in range(4):

        @pl.when(me.c == q % 2)
        def _(q=q):
            for copy in in_core[q]:
                copy.wait_send()

    for side in along:
        for slot in side:
            for copy in slot:
                copy.wait_send()
    for made, start_at in ((carries, first), (more, last_first)):

        @pl.when(me.zh == start_at)
        def _(made=made):
            for copy in made:
                copy.wait_send()

    copies.finish()
    ending.wait_recv()


def local(attn_out, resid, out_proj, section_in, codebook, decays, section_out, codes):
    frames, width = attn_out.shape
    block = out_proj.shape[0]
    _, rows_in, inner = section_in.shape
    code_count = codebook.shape[1]
    chunk = inner // CHUNKS
    rows = frames // 4
    vmem = pl.BlockSpec(memory_space=pltpu.VMEM)
    anywhere = pl.BlockSpec(memory_space=pl.ANY)
    copies = 256
    return pl.pallas_call(
        kernel,
        out_shape=(
            jax.ShapeDtypeStruct((1, frames), F32),
            jax.ShapeDtypeStruct((block, width), BF),
        ),
        in_specs=[vmem, anywhere, vmem, vmem, anywhere, vmem, anywhere, vmem],
        out_specs=[vmem, vmem],
        scratch_shapes=[
            pltpu.VMEM((4, block, frames), BF),
            pltpu.VMEM((4, 4, 2, block, width), BF),
            pltpu.VMEM((frames, width), BF),
            pltpu.VMEM((frames, 8 * width), BF),
            pltpu.VMEM((frames, 8 * width), BF),
            pltpu.VMEM((frames, width), BF),
            pltpu.VMEM((CHUNKS, 4, 4, 2, rows_in, chunk), BF),
            pltpu.VMEM((4, 8, inner), F32),
            pltpu.VMEM((code_count, inner), BF),
            pltpu.VMEM((inner, code_count), BF),
            pltpu.VMEM((frames, inner), F32),
            pltpu.VMEM((CHUNKS, frames, chunk), F32),
            pltpu.VMEM((frames, code_count), F32),
            pltpu.VMEM((frames, code_count), BF),
            pltpu.VMEM((2, CHUNKS, frames, chunk), BF),
            pltpu.VMEM((2, CHUNKS, 4, rows, chunk), BF),
            pltpu.VMEM((2, CHUNKS, 4, rows, chunk), BF),
            pltpu.VMEM((2, CHUNKS, frames, chunk), BF),
            pltpu.VMEM((2, CHUNKS, rows, chunk), BF),
            pltpu.VMEM((2, CHUNKS, rows, chunk), BF),
            pltpu.VMEM((4, 2, 3, frames, block), BF),
            pltpu.VMEM((4, 2, 3, frames, block), BF),
            pltpu.VMEM((4, frames, block), BF),
            pltpu.VMEM((4, frames, block), BF),
            pltpu.VMEM((8, 8, frames), F32),
            pltpu.VMEM((4, 4, 2, block, width), BF),
            pltpu.VMEM((2, 4, 2, block, width), BF),
            pltpu.VMEM((2, 4, 2, block, width), BF),
            pltpu.VMEM((3, 2, 2, block, width), BF),
            pltpu.VMEM((4, block, width), BF),
            pltpu.VMEM((4, block, width), BF),
            pltpu.VMEM((block, width), BF),
            pltpu.SemaphoreType.DMA((copies,)),
            pltpu.SemaphoreType.DMA((copies,)),
            pltpu.SemaphoreType.DMA((3,)),
            pltpu.SemaphoreType.DMA((4,)),
            pltpu.SemaphoreType.DMA((4,)),
        ],
        compiler_params=pltpu.CompilerParams(
            collective_id=0, has_side_effects=True, vmem_limit_bytes=VMEM_LIMIT
        ),
        name="whole",
    )(attn_out, resid, out_proj, section_in[0], codebook[0], decays, section_out[0], codes)


def solution(mesh):
    return jax.shard_map(
        local,
        mesh=mesh,
        in_specs=(
            P("wide", "depth"),
            P("wide", None),
            P("wide", "depth"),
            P("depth", "wide", None),
            P("depth", None, None),
            P("depth", None),
            P("depth", None, None),
            P(None, "wide"),
        ),
        out_specs=(P("depth", "wide"), P("wide", "depth")),
        check_vma=False,
    )
```
